128 devices in a mesh: blk: 32 (over z_hi, y, x), grp: 4 (over z_lo, core).
Axes of the slice: x: 4, y: 4, z: 4 (z_hi: 2, z_lo: 2; z = z_hi * 2 + z_lo), core: 2. Of those that a mesh axis runs over, the one named last changes fastest.
Arguments:
- image_embed: bfloat16 [28672, 512], P(('blk', 'grp')), may hold values from -1 to 1
- text_embed: bfloat16 [28672, 512], P(('blk', 'grp')), may hold values from -1 to 1
Outputs:
- image_grad: float32 [28672, 512], P(('blk', 'grp'))
- text_grad: float32 [28672, 512], P(('blk', 'grp'))
- mean_loss: float32 [1], replicated
The draws below stay inside these ranges and needn't reach their ends.
All inputs are finite; a program needn't handle non-finite values.
Results may differ from the reference program's by a relative error of at most 0.0023.
Values may be sent and summed in bfloat16 or wider, within the bound.
No kernel may reach another device: no remote copies, remote signals or barrier semaphores. Data moves between devices by JAX's collectives and lax.ppermute only.
A program may use at most 128 MiB of HBM per device.

```python
import math
import jax
import jax.numpy as jnp
from jax import lax

D = 512
BATCH = 28672


def common_parts(key):
    key_shared = jax.random.fold_in(key, 0)
    shared = jax.random.normal(key_shared, (BATCH, D), jnp.float32)
    return shared


def assemble(shared, own_noise, spread):
    rising = 3.0 ** (jnp.arange(BATCH, dtype=jnp.float32) / BATCH)
    return (0.7 * shared + 0.7 * own_noise) / math.sqrt(D) * 0.12 * spread * rising[:, None]


def draw_image_embed(key, part):
    shared = common_parts(key)
    key = jax.random.fold_in(key, 17)
    key_noise, key_spread = jax.random.split(key)
    own_noise = jax.random.normal(key_noise, (BATCH, D), jnp.float32)
    spread = jnp.exp(jax.random.uniform(key_spread, (BATCH, 1), jnp.float32) * math.log(4.0))
    vectors = assemble(shared, own_noise, spread)
    return jnp.clip(vectors, -1.0, 1.0).astype(jnp.bfloat16)


def draw_text_embed(key, part):
    shared = common_parts(key)
    key = jax.random.fold_in(key, 29)
    key_noise, key_spread = jax.random.split(key)
    own_noise = jax.random.normal(key_noise, (BATCH, D), jnp.float32)
    spread = jnp.exp(jax.random.uniform(key_spread, (BATCH, 1), jnp.float32) * math.log(4.0))
    vectors = assemble(shared, own_noise, spread)
    return jnp.clip(vectors, -1.0, 1.0).astype(jnp.bfloat16)


def setup_inputs(seed: int = 0) -> dict:
    splits = jax.random.split(jax.random.key(seed), 3)
    return {
        "image_embed": draw_image_embed(jax.random.fold_in(splits[2], 71), 0),
        "text_embed": draw_text_embed(jax.random.fold_in(splits[2], 71), 0),
    }


def reference(image_embed, text_embed):
    batch_rows = image_embed.shape[0]
    stride = 1024 if batch_rows % 1024 == 0 else batch_rows
    block_count = batch_rows // stride
    image_blocks = image_embed.reshape(block_count, stride, D)

    def scores_of(image_block):
        return 100.0 * lax.dot_general(image_block, text_embed, (((1,), (1,)), ((), ())), preferred_element_type=jnp.float32)

    def forward(running, image_block):
        col_max, col_sum = running
        scores = scores_of(image_block)
        row_max = jnp.max(scores, axis=1, keepdims=True)
        row_part = row_max[:, 0] + jnp.log(jnp.sum(jnp.exp(scores - row_max), axis=1))
        new_max = jnp.maximum(col_max, jnp.max(scores, axis=0))
        col_sum = col_sum * jnp.exp(col_max - new_max) + jnp.sum(jnp.exp(scores - new_max[None, :]), axis=0)
        return (new_max, col_sum), row_part

    initial = (jnp.full((batch_rows,), -1e30, jnp.float32), jnp.zeros((batch_rows,), jnp.float32))
    (col_max, col_sum), row_parts = lax.scan(forward, initial, image_blocks)
    row_lse = row_parts.reshape(batch_rows)
    col_lse = col_max + jnp.log(col_sum)
    image_wide = image_embed.astype(jnp.float32)
    text_wide = text_embed.astype(jnp.float32)
    diagonal = 100.0 * jnp.sum(image_wide * text_wide, axis=1)
    mean_loss = (jnp.sum(row_lse - diagonal) + jnp.sum(col_lse - diagonal)) / (2.0 * batch_rows)

    def backward(running, inputs):
        image_block, row_part = inputs
        scores = scores_of(image_block)
        weights = ((jnp.exp(scores - row_part[:, None]) + jnp.exp(scores - col_lse[None, :])) * 0.5).astype(jnp.bfloat16)
        image_part = jnp.dot(weights, text_embed, preferred_element_type=jnp.float32)
        running = running + lax.dot_general(weights, image_block, (((0,), (0,)), ((), ())), preferred_element_type=jnp.float32)
        return running, image_part

    text_sum, image_parts = lax.scan(backward, jnp.zeros((batch_rows, D), jnp.float32), (image_blocks, row_parts))
    image_grad = 100.0 * (image_parts.reshape(batch_rows, D) - text_wide)
    text_grad = 100.0 * (text_sum - image_wide)
    return image_grad, text_grad, mean_loss.reshape(1)
```

```python
import functools
import math

import jax
import jax.numpy as jnp
from jax import lax
from jax.experimental import pallas as pl
from jax.experimental.pallas import tpu as pltpu
from jax.sharding import Mesh, PartitionSpec as P

AXES = ("zh", "y", "x", "zl", "c")
A_AXES = ("y", "zl")
B_AXES = ("zh", "x")
SWAP = [(0, 1), (1, 0)]
LOG2E = math.log2(math.e)
LN2 = math.log(2.0)
SCALE = 100.0 * LOG2E
CHUNK = 256
VMEM_LIMIT = 56 * 1024 * 1024


def forward_kernel(steps, own_ref, other_ref, text_ref, row_ref, col_ref, image, text_t, scores, lse_rows, col_max, col_sum):
    step = pl.program_id(0)
    rows, columns = scores.shape

    @pl.when(step == 0)
    def _():
        text_t[...] = text_ref[...].T
        col_max[...] = jnp.full(col_max.shape, -1e30, jnp.float32)
        col_sum[...] = jnp.zeros(col_sum.shape, jnp.float32)

    @pl.when(step < steps // 2)
    def _():
        image[...] = own_ref[...]

    @pl.when(step >= steps // 2)
    def _():
        image[...] = other_ref[...]

    for start in range(0, columns, CHUNK):
        cols = slice(start, start + CHUNK)
        part = SCALE * jnp.dot(image[...], text_t[:, cols], preferred_element_type=jnp.float32)
        scores[:, cols] = part
        old = col_max[:, cols]
        new = jnp.maximum(old, jnp.max(part.reshape(rows // 8, 8, CHUNK), axis=0))
        col_sum[:, cols] = col_sum[:, cols] * jnp.exp2(old - new)
        col_max[:, cols] = new

    def sums(index, carry):
        at = pl.multiple_of(index * 8, 8)
        block = scores[pl.ds(at, 8), :]
        pieces = [block[:, k : k + 128] for k in range(0, columns, 128)]
        row_max = functools.reduce(jnp.maximum, pieces)
        row_sum = functools.reduce(jnp.add, [jnp.exp2(piece - row_max) for piece in pieces])
        peak = jnp.max(row_max, axis=1, keepdims=True)
        total = jnp.sum(row_sum * jnp.exp2(row_max - peak), axis=1, keepdims=True)
        lse_rows[pl.ds(at, 8), :] = jnp.broadcast_to(peak + jnp.log2(total), (8, 128))
        return carry + jnp.exp2(block - col_max[...])

    col_sum[...] = lax.fori_loop(0, rows // 8, sums, col_sum[...], unroll=4)
    row_ref[...] = lse_rows[...].T[:8, :]

    @pl.when(step == steps - 1)
    def _():
        peak = jnp.max(col_max[...], axis=0, keepdims=True)
        total = jnp.sum(col_sum[...] * jnp.exp2(col_max[...] - peak), axis=0, keepdims=True)
        col_ref[...] = jnp.broadcast_to(peak + jnp.log2(total), col_ref.shape)


def forward(own, other, text):
    half, width = own.shape
    columns = text.shape[0]
    rows = half // 2
    steps = 4
    elements = 2 * half * columns
    return pl.pallas_call(
        functools.partial(forward_kernel, steps),
        grid=(steps,),
        in_specs=[
            pl.BlockSpec((rows, width), lambda i: (jnp.minimum(i, 1), 0)),
            pl.BlockSpec((rows, width), lambda i: (jnp.maximum(i - 2, 0), 0)),
            pl.BlockSpec((columns, width), lambda i: (0, 0)),
        ],
        out_specs=[
            pl.BlockSpec((8, rows), lambda i: (0, i)),
            pl.BlockSpec((8, columns), lambda i: (0, 0)),
        ],
        out_shape=[
            jax.ShapeDtypeStruct((8, 2 * half), jnp.float32),
            jax.ShapeDtypeStruct((8, columns), jnp.float32),
        ],
        scratch_shapes=[
            pltpu.VMEM((rows, width), jnp.bfloat16),
            pltpu.VMEM((width, columns), jnp.bfloat16),
            pltpu.VMEM((rows, columns), jnp.float32),
            pltpu.VMEM((rows, 128), jnp.float32),
            pltpu.VMEM((8, columns), jnp.float32),
            pltpu.VMEM((8, columns), jnp.float32),
        ],
        compiler_params=pltpu.CompilerParams(vmem_limit_bytes=VMEM_LIMIT),
        cost_estimate=pl.CostEstimate(
            flops=2 * elements * width, bytes_accessed=4 * (half + columns) * width, transcendentals=2 * elements
        ),
    )(own, other, text)


def backward_kernel(steps, last, image_ref, text_ref, row_ref, col_ref, *rest):
    if last:
        text_in, image_out, text_out, image_t, text_t, weights, row_lse, total = rest
    else:
        image_out, text_out, image_t, text_t, weights, row_lse, total = rest
    step = pl.program_id(0)
    rows, columns = weights.shape

    @pl.when(step == 0)
    def _():
        text_t[...] = text_ref[...].T
        total[...] = text_in[...] if last else jnp.zeros(total.shape, jnp.float32)

    image_t[...] = image_ref[...].T
    row_lse[...] = jnp.broadcast_to(row_ref[0:1, :], (128, rows)).T
    for start in range(0, columns, CHUNK):
        cols = slice(start, start + CHUNK)
        part = SCALE * jnp.dot(image_ref[...], text_t[:, cols], preferred_element_type=jnp.float32)
        row_part = jnp.concatenate([row_lse[...]] * (CHUNK // 128), axis=1)
        value = (jnp.exp2(part - row_part) + jnp.exp2(part - col_ref[0:1, cols])).astype(jnp.bfloat16)
        weights[:, cols] = value
        total[:, cols] += jnp.dot(image_t[...], value, preferred_element_type=jnp.float32)
    image_sum = jnp.dot(weights[...], text_ref[...], preferred_element_type=jnp.float32)
    image_out[...] = image_sum.astype(image_out.dtype)

    @pl.when(step == steps - 1)
    def _():
        text_out[...] = total[...].T if last else total[...]


def backward(image, text, row_lse, col_lse, text_in):
    half, width = image.shape
    columns = text.shape[0]
    rows = half // 2
    steps = 2
    last = text_in is not None
    elements = half * columns
    whole = lambda shape: pl.BlockSpec(shape, lambda i: (0, 0))
    extra = [whole((width, columns))] if last else []
    text_shape = (columns, width) if last else (width, columns)
    return pl.pallas_call(
        functools.partial(backward_kernel, steps, last),
        grid=(steps,),
        in_specs=[
            pl.BlockSpec((rows, width), lambda i: (i, 0)),
            whole((columns, width)),
            pl.BlockSpec((8, rows), lambda i: (0, i)),
            whole((8, columns)),
        ]
        + extra,
        out_specs=[pl.BlockSpec((rows, width), lambda i: (i, 0)), whole(text_shape)],
        out_shape=[
            jax.ShapeDtypeStruct((half, width), jnp.float32 if last else jnp.bfloat16),
            jax.ShapeDtypeStruct(text_shape, jnp.float32),
        ],
        scratch_shapes=[
            pltpu.VMEM((width, rows), jnp.bfloat16),
            pltpu.VMEM((width, columns), jnp.bfloat16),
            pltpu.VMEM((rows, columns), jnp.bfloat16),
            pltpu.VMEM((rows, 128), jnp.float32),
            pltpu.VMEM((width, columns), jnp.float32),
        ],
        compiler_params=pltpu.CompilerParams(vmem_limit_bytes=VMEM_LIMIT),
        cost_estimate=pl.CostEstimate(
            flops=6 * elements * width, bytes_accessed=8 * (half + columns) * width, transcendentals=2 * elements
        ),
    )(image, text, row_lse, col_lse, *([text_in] if last else []))


def to_all(value, axes):
    count = math.prod(lax.axis_size(axis) for axis in axes)
    copies = jnp.broadcast_to(value[None], (count,) + value.shape)
    return lax.all_to_all(copies, axes, split_axis=0, concat_axis=0, tiled=True)


def joined(first, second):
    peak = jnp.maximum(first, second)
    return peak + jnp.log2(jnp.exp2(first - peak) + jnp.exp2(second - peak))


def joined_all(parts):
    peak = jnp.max(parts, axis=0)
    return peak + jnp.log2(jnp.sum(jnp.exp2(parts - peak[None]), axis=0))


def with_scalar(blocks, scalar):
    count, rows, width = blocks.shape
    high = lax.reduce_precision(scalar, 8, 7)
    middle = lax.reduce_precision(scalar - high, 8, 7)
    low = scalar - high - middle
    lane = lax.broadcasted_iota(jnp.int32, (count, 16, width), 2)
    extra = jnp.where(lane == 0, high, jnp.where(lane == 1, middle, jnp.where(lane == 2, low, 0.0)))
    return jnp.concatenate([blocks.astype(jnp.bfloat16), extra.astype(jnp.bfloat16)], axis=1)


def summed(blocks, scalar, axes, own, index):
    rows = blocks.shape[1]
    parts = lax.all_to_all(with_scalar(blocks, scalar), axes, split_axis=0, concat_axis=0, tiled=True)
    place = lax.broadcasted_iota(jnp.int32, (blocks.shape[0], 1, 1), 0)
    others = jnp.where(place == index, 0.0, parts[:, :rows].astype(jnp.float32))
    return own + jnp.sum(others, axis=0), jnp.sum(parts[:, rows, :3].astype(jnp.float32))


def body(image_embed, text_embed):
    rows, width = image_embed.shape
    count_a = math.prod(lax.axis_size(axis) for axis in A_AXES)
    count_b = math.prod(lax.axis_size(axis) for axis in B_AXES)
    index_a = lax.axis_index(A_AXES)
    index_b = lax.axis_index(B_AXES)
    batch = rows * 2 * count_a * count_b

    own = to_all(image_embed, A_AXES).reshape(count_a * rows, width)
    other = lax.ppermute(own, "c", SWAP)
    text = to_all(text_embed, B_AXES).reshape(count_b * rows, width)

    row_part, col_part = forward(own, other, text)

    own_image = image_embed.astype(jnp.float32)
    own_text = text_embed.astype(jnp.float32)
    diagonal = 100.0 * jnp.sum(own_image * own_text)
    half = count_a * rows
    row_part = row_part[0].reshape(2, half // 128, 128)
    swapped, diagonal_swapped = lax.ppermute((row_part, jnp.full((8, 128), diagonal)), "c", SWAP)
    row_part = joined(row_part, swapped[::-1]).reshape(2 * half // 128, 128)
    diagonal_row = jnp.full((1, 128), diagonal) + diagonal_swapped[:1]
    from_a = to_all(jnp.concatenate([row_part, diagonal_row], axis=0), A_AXES)
    from_b = to_all(col_part[0].reshape(-1, 128), B_AXES)
    row_lse = joined_all(from_a[:, :-1]).reshape(1, 2 * half)
    col_lse = joined_all(from_b).reshape(1, count_b * rows)
    term_b = LN2 * (jnp.sum(row_lse[:, :half]) + jnp.sum(row_lse[:, half:])) - 2.0 * jnp.sum(from_a[:, -1, 0])
    term_c = LN2 * jnp.sum(col_lse)
    term_a = term_c + lax.ppermute(jnp.full((8, 128), term_c), "c", SWAP)[0, 0]

    row_eight = jnp.broadcast_to(row_lse + 1.0, (8, 2 * half))
    col_eight = jnp.broadcast_to(col_lse + 1.0, (8, count_b * rows))
    image_other, text_half = backward(other, text, row_eight[:, half:], col_eight, None)
    image_back = lax.ppermute(image_other, "c", SWAP)
    image_own, text_sum = backward(own, text, row_eight[:, :half], col_eight, text_half)

    text_blocks = text_sum.reshape(count_b, rows, width)
    text_own = lax.dynamic_index_in_dim(text_blocks, index_b, 0, keepdims=False)
    text_total, loss_b = summed(text_blocks, term_b, B_AXES, text_own, index_b)
    image_blocks = (image_own + image_back.astype(jnp.float32)).reshape(count_a, rows, width)
    image_part = lax.dynamic_index_in_dim(image_blocks, index_a, 0, keepdims=False)
    image_total, loss_a = summed(image_blocks, term_a, A_AXES, image_part, index_a)

    image_grad = 100.0 * (image_total - own_text)
    text_grad = 100.0 * (text_total - own_image)
    mean_loss = (loss_a + loss_b) / (2.0 * batch)
    return (image_grad, text_grad, mean_loss.reshape(1))


def solution(mesh):
    fine = Mesh(mesh.devices.reshape(2, 4, 4, 2, 2), AXES)
    spec = P(AXES, None)
    return jax.shard_map(body, mesh=fine, in_specs=(spec, spec), out_specs=(spec, spec, P()), check_vma=False)
```

```python
import functools
import itertools
import math

import jax
import jax.numpy as jnp
from jax import lax
from jax.experimental import pallas as pl
from jax.experimental.pallas import tpu as pltpu
from jax.sharding import Mesh, PartitionSpec as P

AXES = ("zh", "y", "x", "zl", "c")
A_BITS = ("zp", "yq", "yp")
B_BITS = ("zq", "xq", "xp")
PAIRS = ((0, 0), (1, 0), (1, 1), (0, 1))
SWAP = [(0, 1), (1, 0)]
LOG2E = math.log2(math.e)
LN2 = math.log(2.0)
SCALE = 100.0 * LOG2E
BLOCK = 256
TAIL = 16
VMEM_LIMIT = 56 * 1024 * 1024


def forward_kernel(own_ref, other_ref, text_ref, image_ref, pair_ref, row_ref, col_ref, text_t, image, scores, block_max, row_max, row_sum, col_max, col_sum):
    half = own_ref.shape[0]
    columns = text_ref.shape[0]
    count = 2 * half // BLOCK
    text_t[...] = text_ref[...].T
    image[:half, :] = own_ref[...]
    image[half:, :] = other_ref[...]
    col_max[...] = jnp.full(col_max.shape, -1e30, jnp.float32)
    col_sum[...] = jnp.zeros(col_sum.shape, jnp.float32)

    def multiply(index, slot):
        at = pl.multiple_of(jnp.minimum(index, count - 1) * BLOCK, BLOCK)
        rows = image[pl.ds(at, BLOCK), :]
        for start in range(0, columns, BLOCK):
            cols = slice(start, start + BLOCK)
            part = SCALE * jnp.dot(rows, text_t[:, cols], preferred_element_type=jnp.float32)
            scores[slot][:, cols] = part
            block_max[slot][:, cols] = jnp.max(part.reshape(BLOCK // 8, 8, BLOCK), axis=0)

    def sums(index, slot):
        old = col_max[...]
        peak = jnp.maximum(old, block_max[slot][...])
        col_max[...] = peak
        total = col_sum[...] * jnp.exp2(old - peak)
        for start in range(0, BLOCK, 8):
            block = scores[slot][start : start + 8, :]
            pieces = [block[:, k : k + 128] for k in range(0, columns, 128)]
            top = functools.reduce(jnp.maximum, pieces)
            at = pl.multiple_of(index * BLOCK + start, 8)
            row_max[pl.ds(at, 8), :] = top
            row_sum[pl.ds(at, 8), :] = functools.reduce(jnp.add, [jnp.exp2(piece - top) for piece in pieces])
            total = total + jnp.exp2(block - peak)
        col_sum[...] = total

    multiply(0, 0)

    @pl.loop(0, count // 2)
    def _(turn):
        multiply(2 * turn + 1, 1)
        sums(2 * turn, 0)
        multiply(2 * turn + 2, 0)
        sums(2 * turn + 1, 1)

    tops = row_max[...].T
    parts = row_sum[...].T
    peak = jnp.max(tops, axis=0, keepdims=True)
    total = jnp.sum(parts * jnp.exp2(tops - peak), axis=0, keepdims=True)
    row_lse = peak + jnp.log2(total)
    for k in range(2 * half // 128):
        row_ref[k : k + 1, :] = row_lse[:, k * 128 : k * 128 + 128]
    peak = jnp.max(col_max[...], axis=0, keepdims=True)
    total = jnp.sum(col_sum[...] * jnp.exp2(col_max[...] - peak), axis=0, keepdims=True)
    col_lse = peak + jnp.log2(total)
    products = image_ref[...].astype(jnp.float32) * pair_ref[...].astype(jnp.float32)
    diagonal = 100.0 * jnp.sum(jnp.sum(products, axis=0, keepdims=True), axis=1, keepdims=True)
    count = columns // 128
    for place in range(col_ref.shape[0]):
        for k in range(count):
            col_ref[place, k : k + 1, :] = col_lse[:, k * 128 : k * 128 + 128]
        col_ref[place, count:, :] = jnp.broadcast_to(diagonal, (col_ref.shape[1] - count, 128))


def forward(own, other, text, image, pair, members):
    half, width = own.shape
    columns = text.shape[0]
    elements = 2 * half * columns
    f32 = lambda *shape: pltpu.VMEM(shape, jnp.float32)
    return pl.pallas_call(
        forward_kernel,
        out_shape=[
            jax.ShapeDtypeStruct((2 * half // 128, 128), jnp.float32),
            jax.ShapeDtypeStruct((members, columns // 128 + 2, 128), jnp.float32),
        ],
        scratch_shapes=[
            pltpu.VMEM((width, columns), jnp.bfloat16),
            pltpu.VMEM((2 * half, width), jnp.bfloat16),
            [f32(BLOCK, columns), f32(BLOCK, columns)],
            [f32(8, columns), f32(8, columns)],
            f32(2 * half, 128),
            f32(2 * half, 128),
            f32(8, columns),
            f32(8, columns),
        ],
        compiler_params=pltpu.CompilerParams(vmem_limit_bytes=VMEM_LIMIT),
        cost_estimate=pl.CostEstimate(
            flops=2 * elements * width, bytes_accessed=4 * (half + columns) * width, transcendentals=2 * elements
        ),
    )(own, other, text, image, pair)


def tail_of(scalar, width):
    spread = jnp.broadcast_to(scalar, (TAIL, width))
    high = spread.astype(jnp.bfloat16).astype(jnp.float32)
    middle = (spread - high).astype(jnp.bfloat16).astype(jnp.float32)
    low = spread - high - middle
    lane = lax.broadcasted_iota(jnp.int32, (TAIL, width), 1)
    values = jnp.where(lane == 0, high, jnp.where(lane == 1, middle, jnp.where(lane == 2, low, 0.0)))
    return values.astype(jnp.bfloat16)


def whole_lse(parts_ref, lse_ref):
    count = lse_ref.shape[1] // 128
    parts = parts_ref[:, :count, :]
    peak = jnp.max(parts, axis=0)
    value = peak + jnp.log2(jnp.sum(jnp.exp2(parts - peak[None]), axis=0)) + 1.0
    for k in range(count):
        lse_ref[:, k * 128 : k * 128 + 128] = jnp.broadcast_to(value[k : k + 1, :], (8, 128))


def gradient_kernel(pieces, pack, offset, *refs):
    if pack:
        index_ref, *refs = refs
    row_ref, col_ref, rows_ref, *refs = refs
    column_refs, refs = refs[:pieces], refs[pieces:]
    if pack:
        out_ref, own_ref, row_parts, col_parts = refs[0], refs[1], row_ref, col_ref
        row_ref, col_ref, *refs = refs[2:]
        whole_lse(row_parts, row_ref)
        whole_lse(col_parts, col_ref)
    else:
        out_ref, *refs = refs
    columns_t, columns, scores, weights, row_lse, tail = refs
    total = rows_ref.shape[0]
    block = weights[0].shape[0]
    count = total // block
    size = column_refs[0].shape[0]
    for piece in range(pieces):
        part = slice(piece * size, (piece + 1) * size)
        columns_t[:, part] = column_refs[piece][...].T
        columns[part, :] = column_refs[piece][...]
    across = columns.shape[0]
    row_lse[...] = jnp.broadcast_to(row_ref[0:1, offset : offset + total], (128, total)).T
    if pack:
        halves = [col_ref[0:1, : across // 2], col_ref[0:1, across // 2 :]]
        sums = [jnp.sum(half - 1.0, axis=1, keepdims=True) for half in halves]
        tail[...] = tail_of(LN2 * (sums[0] + sums[1]), tail.shape[1])

    def multiply(index, slot):
        rows = rows_ref[pl.ds(pl.multiple_of(index * block, block), block), :]
        for start in range(0, across, BLOCK):
            cols = slice(start, start + BLOCK)
            scores[slot][:, cols] = jnp.dot(rows, columns_t[:, cols], preferred_element_type=jnp.float32)

    def weigh(index, slot):
        row_part = row_lse[pl.ds(pl.multiple_of(index * block, block), block), :]
        for start in range(0, across, 128):
            cols = slice(start, start + 128)
            scaled = SCALE * scores[slot][:, cols]
            value = jnp.exp2(scaled - row_part) + jnp.exp2(scaled - col_ref[0:1, cols])
            weights[slot][:, cols] = value.astype(jnp.bfloat16)

    def collect(index, slot):
        value = jnp.dot(weights[slot][...], columns[...], preferred_element_type=jnp.float32)
        if not pack:
            out_ref[pl.ds(pl.multiple_of(index * block, block), block), :] = value.astype(out_ref.dtype)
            return
        mine = index == index_ref[0]
        at = pl.multiple_of(index * (block + TAIL), TAIL)
        out_ref[pl.ds(at, block), :] = jnp.where(mine, 0.0, value).astype(out_ref.dtype)
        out_ref[pl.ds(pl.multiple_of(at + block, TAIL), TAIL), :] = tail[...]

        @pl.when(mine)
        def _():
            own_ref[...] = value

    multiply(0, 0)
    multiply(1, 1)
    weigh(0, 0)

    @pl.loop(0, count // 2 - 1)
    def _(turn):
        multiply(2 * turn + 2, 0)
        collect(2 * turn, 0)
        weigh(2 * turn + 1, 1)
        multiply(2 * turn + 3, 1)
        collect(2 * turn + 1, 1)
        weigh(2 * turn + 2, 0)

    collect(count - 2, 0)
    weigh(count - 1, 1)
    collect(count - 1, 1)


def gradient(rows, columns, row_lse, col_lse, block, index=None, offset=0, dtype=jnp.bfloat16):
    total, width = rows.shape
    across = sum(piece.shape[0] for piece in columns)
    elements = total * across
    pack = index is not None
    vmem = pl.BlockSpec(memory_space=pltpu.VMEM)
    smem = pl.BlockSpec(memory_space=pltpu.SMEM)
    if pack:
        out_shape = [
            jax.ShapeDtypeStruct((total // block * (block + TAIL), width), jnp.bfloat16),
            jax.ShapeDtypeStruct((block, width), jnp.float32),
            jax.ShapeDtypeStruct((8, total), jnp.float32),
            jax.ShapeDtypeStruct((8, across), jnp.float32),
        ]
    else:
        out_shape = jax.ShapeDtypeStruct((total, width), dtype)
    return pl.pallas_call(
        functools.partial(gradient_kernel, len(columns), pack, offset),
        in_specs=([smem] if pack else []) + [vmem] * (3 + len(columns)),
        out_shape=out_shape,
        scratch_shapes=[
            pltpu.VMEM((width, across), jnp.bfloat16),
            pltpu.VMEM((across, width), jnp.bfloat16),
            [pltpu.VMEM((block, across), jnp.float32)] * 2,
            [pltpu.VMEM((block, across), jnp.bfloat16)] * 2,
            pltpu.VMEM((total, 128), jnp.float32),
            pltpu.VMEM((TAIL, width), jnp.bfloat16),
        ],
        compiler_params=pltpu.CompilerParams(vmem_limit_bytes=VMEM_LIMIT),
        cost_estimate=pl.CostEstimate(
            flops=4 * elements * width if pack else 0, bytes_accessed=4 * (total + across) * width, transcendentals=0
        ),
    )(*([index] if pack else []), row_lse, col_lse, rows, *columns)


def pack_kernel(index_ref, term_ref, own_ref, back_ref, out_ref, mine_ref):
    rows = own_ref.shape[0]
    mine = pl.program_id(0) == index_ref[0]
    value = own_ref[...] + back_ref[...].astype(jnp.float32)
    out_ref[:rows, :] = jnp.where(mine, 0.0, value).astype(out_ref.dtype)
    out_ref[rows:, :] = tail_of(term_ref[0], out_ref.shape[1])

    @pl.when(mine)
    def _():
        mine_ref[...] = value


def packed(own, back, block, index, term):
    total, width = own.shape
    rows = pl.BlockSpec((block, width), lambda i: (i, 0))
    return pl.pallas_call(
        pack_kernel,
        grid=(total // block,),
        in_specs=[
            pl.BlockSpec(memory_space=pltpu.SMEM),
            pl.BlockSpec(memory_space=pltpu.SMEM),
            rows,
            rows,
        ],
        out_specs=[
            pl.BlockSpec((block + TAIL, width), lambda i: (i, 0)),
            pl.BlockSpec((block, width), lambda i: (0, 0)),
        ],
        out_shape=[
            jax.ShapeDtypeStruct((total // block * (block + TAIL), width), jnp.bfloat16),
            jax.ShapeDtypeStruct((block, width), jnp.float32),
        ],
        compiler_params=pltpu.CompilerParams(vmem_limit_bytes=VMEM_LIMIT),
    )(index, term.reshape(1), own, back)


def finish_kernel(parts_ref, own_ref, pair_ref, grad_ref, scalar_ref):
    count = parts_ref.shape[0]
    rows = own_ref.shape[0]
    value = own_ref[...] - pair_ref[...].astype(jnp.float32)
    tail = jnp.zeros((TAIL, own_ref.shape[1]), jnp.float32)
    for part in range(count):
        value = value + parts_ref[part, :rows, :].astype(jnp.float32)
        tail = tail + parts_ref[part, rows:, :].astype(jnp.float32)
    grad_ref[...] = 100.0 * value
    scalar_ref[...] = tail


def finished(parts, own, pair):
    return pl.pallas_call(
        finish_kernel,
        out_shape=[
            jax.ShapeDtypeStruct(own.shape, jnp.float32),
            jax.ShapeDtypeStruct((TAIL, own.shape[1]), jnp.float32),
        ],
        compiler_params=pltpu.CompilerParams(vmem_limit_bytes=VMEM_LIMIT),
    )(parts, own, pair)


def bits_of(x, y, z):
    return {axis + kind: PAIRS[at][k] for axis, at in zip("xyz", (x, y, z)) for k, kind in enumerate("pq")}


def groups_of(names):
    found = {}
    for z, y, x, core in itertools.product(range(4), range(4), range(4), range(2)):
        bits = bits_of(x, y, z)
        key = tuple(bits[name] for name in sorted(bits) if name not in names) + (core,)
        place = functools.reduce(lambda total, name: 2 * total + bits[name], names, 0)
        found.setdefault(key, {})[place] = ((((z // 2) * 4 + y) * 4 + x) * 2 + z % 2) * 2 + core
    return [[group[place] for place in sorted(group)] for group in found.values()]


def own_bits():
    where = {"x": lax.axis_index("x"), "y": lax.axis_index("y"), "z": 2 * lax.axis_index("zh") + lax.axis_index("zl")}
    bits = {}
    for axis, at in where.items():
        bits[axis + "p"] = jnp.where((at == 1) | (at == 2), 1, 0)
        bits[axis + "q"] = at // 2
    return bits


def place_of(names, bits):
    return functools.reduce(lambda total, name: 2 * total + bits[name], names, 0)


def doubled(value, names, name, bits):
    mask = 1 << (len(names) - 1 - names.index(name))
    pairs = [(group[at], group[at ^ mask]) for group in groups_of(names) for at in range(len(group))]
    back = lax.ppermute(value, AXES, pairs)
    at = lax.broadcasted_iota(jnp.int32, (2,) + (1,) * value.ndim, 0)
    return jnp.where(at == bits[name], value[None], back[None])


def gathered(image, text, bits):
    half = image.shape[0] // 2
    pieces = [image[:half], image[half:], text[:half], text[half:]]
    names = [A_BITS, A_BITS, B_BITS, B_BITS]
    for turn in range(3):
        pieces = [
            doubled(piece, name, name[2 - turn] if k % 2 == 0 else name[2 - (2, 0, 1)[turn]], bits)
            for k, (piece, name) in enumerate(zip(pieces, names))
        ]
    whole = []
    for k in (0, 2):
        both = jnp.stack([pieces[k], jnp.transpose(pieces[k + 1], (2, 0, 1, 3, 4))], axis=3)
        whole.append(both.reshape(16 * half, image.shape[1]))
    return lax.optimization_barrier(tuple(whole))


def swap(value):
    return lax.ppermute(value, "c", [(0, 1), (1, 0)])


def exchanged(blocks, names):
    return lax.all_to_all(
        blocks, AXES, split_axis=0, concat_axis=0, tiled=True, axis_index_groups=groups_of(names)
    )


def joined(first, second):
    peak = jnp.maximum(first, second)
    return peak + jnp.log2(jnp.exp2(first - peak) + jnp.exp2(second - peak))


def body(image_embed, text_embed):
    rows, width = image_embed.shape
    bits = own_bits()
    members = 2 ** len(A_BITS)
    half = members * rows
    batch = rows * 2 * members * members
    at_a = jnp.full((1,), place_of(A_BITS, bits), jnp.int32)
    at_b = jnp.full((1,), place_of(B_BITS, bits), jnp.int32)

    own, text = gathered(image_embed, text_embed, bits)
    other = swap(own)
    row_part, col_parts = forward(own, other, text, image_embed, text_embed, members)

    col_parts = exchanged(col_parts, B_BITS)
    row_part = row_part.reshape(2, half // 128, 128)
    row_part = joined(row_part, swap(row_part)[::-1]).reshape(1, 2 * half // 128, 128)
    row_parts = exchanged(jnp.broadcast_to(row_part, (members,) + row_part.shape[1:]), A_BITS)

    text_sum, text_own, col_lse, row_lse = gradient(text, [own, other], col_parts, row_parts, rows, at_b)
    term_c = LN2 * jnp.sum(col_lse[0] - 1.0) - 2.0 * jnp.sum(col_parts[:, -1, 0])
    text_sum, own, other = lax.optimization_barrier((text_sum, own, other))
    text_parts = exchanged(text_sum.reshape(members, rows + TAIL, width), B_BITS)
    image_other = gradient(other, [text], row_lse, col_lse, rows, offset=half)
    image_back = swap(image_other)
    image_half = gradient(own, [text], row_lse, col_lse, rows, dtype=jnp.float32)
    term_a = term_c + swap(jnp.full((8, 128), term_c))[0, 0]
    image_sum, image_own = packed(image_half, image_back, rows, at_a, term_a)
    image_parts = exchanged(image_sum.reshape(members, rows + TAIL, width), A_BITS)
    text_grad, tail_b = finished(text_parts, text_own, image_embed)
    image_grad, tail_a = finished(image_parts, image_own, text_embed)
    mean_loss = (jnp.sum(tail_a[0, :3]) + jnp.sum(tail_b[0, :3])) / (2.0 * batch)
    return (image_grad, text_grad, mean_loss.reshape(1))


def solution(mesh):
    fine = Mesh(mesh.devices.reshape(2, 4, 4, 2, 2), AXES)
    spec = P(AXES, None)
    return jax.shard_map(body, mesh=fine, in_specs=(spec, spec), out_specs=(spec, spec, P()), check_vma=False)
```

```python
import functools
import itertools
import math

import jax
import jax.numpy as jnp
from jax import lax
from jax.experimental import pallas as pl
from jax.experimental.pallas import tpu as pltpu
from jax.sharding import Mesh, PartitionSpec as P

AXES = ("zh", "y", "x", "zl", "c")
A_BITS = ("zp", "yq", "yp")
B_BITS = ("zq", "xq", "xp")
PAIRS = ((0, 0), (1, 0), (1, 1), (0, 1))
SWAP = [(0, 1), (1, 0)]
LOG2E = math.log2(math.e)
LN2 = math.log(2.0)
SCALE = 100.0 * LOG2E
BLOCK = 256
TAIL = 16
TEXT_BLOCKS = 1
IMAGE_BLOCKS = 2
VMEM_LIMIT = 56 * 1024 * 1024


def forward_kernel(own_ref, other_ref, text_ref, image_ref, pair_ref, row_ref, col_ref, text_t, image, scores, block_max, row_max, row_sum, col_max, col_sum):
    half = own_ref.shape[0]
    columns = text_ref.shape[0]
    count = 2 * half // BLOCK
    text_t[...] = text_ref[...].T
    image[:half, :] = own_ref[...]
    image[half:, :] = other_ref[...]
    col_max[...] = jnp.full(col_max.shape, -1e30, jnp.float32)
    col_sum[...] = jnp.zeros(col_sum.shape, jnp.float32)

    def multiply(index, slot):
        at = pl.multiple_of(jnp.minimum(index, count - 1) * BLOCK, BLOCK)
        rows = image[pl.ds(at, BLOCK), :]
        for start in range(0, columns, BLOCK):
            cols = slice(start, start + BLOCK)
            part = SCALE * jnp.dot(rows, text_t[:, cols], preferred_element_type=jnp.float32)
            scores[slot][:, cols] = part
            block_max[slot][:, cols] = jnp.max(part.reshape(BLOCK // 8, 8, BLOCK), axis=0)

    def sums(index, slot):
        old = col_max[...]
        peak = jnp.maximum(old, block_max[slot][...])
        col_max[...] = peak
        total = col_sum[...] * jnp.exp2(old - peak)
        for start in range(0, BLOCK, 8):
            block = scores[slot][start : start + 8, :]
            pieces = [block[:, k : k + 128] for k in range(0, columns, 128)]
            top = functools.reduce(jnp.maximum, pieces)
            at = pl.multiple_of(index * BLOCK + start, 8)
            row_max[pl.ds(at, 8), :] = top
            row_sum[pl.ds(at, 8), :] = functools.reduce(jnp.add, [jnp.exp2(piece - top) for piece in pieces])
            total = total + jnp.exp2(block - peak)
        col_sum[...] = total

    multiply(0, 0)

    @pl.loop(0, count // 2)
    def _(turn):
        multiply(2 * turn + 1, 1)
        sums(2 * turn, 0)
        multiply(2 * turn + 2, 0)
        sums(2 * turn + 1, 1)

    tops = row_max[...].T
    parts = row_sum[...].T
    peak = jnp.max(tops, axis=0, keepdims=True)
    total = jnp.sum(parts * jnp.exp2(tops - peak), axis=0, keepdims=True)
    row_lse = peak + jnp.log2(total)
    for k in range(2 * half // 128):
        row_ref[k : k + 1, :] = row_lse[:, k * 128 : k * 128 + 128]
    peak = jnp.max(col_max[...], axis=0, keepdims=True)
    total = jnp.sum(col_sum[...] * jnp.exp2(col_max[...] - peak), axis=0, keepdims=True)
    col_lse = peak + jnp.log2(total)
    products = image_ref[...].astype(jnp.float32) * pair_ref[...].astype(jnp.float32)
    diagonal = 100.0 * jnp.sum(jnp.sum(products, axis=0, keepdims=True), axis=1, keepdims=True)
    count = columns // 128
    for place in range(col_ref.shape[0]):
        for k in range(count):
            col_ref[place, k : k + 1, :] = col_lse[:, k * 128 : k * 128 + 128]
        col_ref[place, count:, :] = jnp.broadcast_to(diagonal, (col_ref.shape[1] - count, 128))


def forward(own, other, text, image, pair, members):
    half, width = own.shape
    columns = text.shape[0]
    elements = 2 * half * columns
    f32 = lambda *shape: pltpu.VMEM(shape, jnp.float32)
    return pl.pallas_call(
        forward_kernel,
        out_shape=[
            jax.ShapeDtypeStruct((2 * half // 128, 128), jnp.float32),
            jax.ShapeDtypeStruct((members, columns // 128 + 2, 128), jnp.float32),
        ],
        scratch_shapes=[
            pltpu.VMEM((width, columns), jnp.bfloat16),
            pltpu.VMEM((2 * half, width), jnp.bfloat16),
            [f32(BLOCK, columns), f32(BLOCK, columns)],
            [f32(8, columns), f32(8, columns)],
            f32(2 * half, 128),
            f32(2 * half, 128),
            f32(8, columns),
            f32(8, columns),
        ],
        compiler_params=pltpu.CompilerParams(vmem_limit_bytes=VMEM_LIMIT),
        cost_estimate=pl.CostEstimate(
            flops=2 * elements * width, bytes_accessed=4 * (half + columns) * width, transcendentals=2 * elements
        ),
    )(own, other, text, image, pair)


def tail_of(scalar, width):
    spread = jnp.broadcast_to(scalar, (TAIL, width))
    high = spread.astype(jnp.bfloat16).astype(jnp.float32)
    middle = (spread - high).astype(jnp.bfloat16).astype(jnp.float32)
    low = spread - high - middle
    lane = lax.broadcasted_iota(jnp.int32, (TAIL, width), 1)
    values = jnp.where(lane == 0, high, jnp.where(lane == 1, middle, jnp.where(lane == 2, low, 0.0)))
    return values.astype(jnp.bfloat16)


def whole_lse(parts_ref, lse_ref):
    count = lse_ref.shape[1] // 128
    parts = parts_ref[:, :count, :]
    peak = jnp.max(parts, axis=0)
    value = peak + jnp.log2(jnp.sum(jnp.exp2(parts - peak[None]), axis=0)) + 1.0
    for k in range(count):
        lse_ref[:, k * 128 : k * 128 + 128] = jnp.broadcast_to(value[k : k + 1, :], (8, 128))


def gradient_kernel(unit, pack, *refs):
    if pack:
        index_ref, row_parts, col_parts, rows_ref, first_ref, second_ref, *refs = refs
        out_ref, own_ref, row_ref, col_ref, *refs = refs
        whole_lse(row_parts, row_ref)
        whole_lse(col_parts, col_ref)
        column_refs = (first_ref, second_ref)
    else:
        row_ref, col_ref, own_rows, other_rows, column_ref, *refs = refs
        own_ref, other_ref, rows_ref, *refs = refs
        rows_ref[: other_rows.shape[0], :] = other_rows[...]
        rows_ref[other_rows.shape[0] :, :] = own_rows[...]
        column_refs = (column_ref,)
    columns_t, columns, scores, weights, row_lse, tail = refs
    total = rows_ref.shape[0]
    block = weights[0].shape[0]
    count = total // block
    size = column_refs[0].shape[0]
    for piece, column_ref in enumerate(column_refs):
        part = slice(piece * size, (piece + 1) * size)
        columns_t[:, part] = column_ref[...].T
        columns[part, :] = column_ref[...]
    across = columns.shape[0]
    if pack:
        row_lse[...] = jnp.broadcast_to(row_ref[0:1, :], (128, total)).T
        halves = [col_ref[0:1, : across // 2], col_ref[0:1, across // 2 :]]
        sums = [jnp.sum(half - 1.0, axis=1, keepdims=True) for half in halves]
        tail[...] = tail_of(LN2 * (sums[0] + sums[1]), tail.shape[1])
    else:
        row_lse[: total // 2, :] = jnp.broadcast_to(row_ref[0:1, total // 2 :], (128, total // 2)).T
        row_lse[total // 2 :, :] = jnp.broadcast_to(row_ref[0:1, : total // 2], (128, total // 2)).T

    def multiply(index, slot):
        rows = rows_ref[pl.ds(pl.multiple_of(index * block, block), block), :]
        for start in range(0, across, BLOCK):
            cols = slice(start, start + BLOCK)
            scores[slot][:, cols] = jnp.dot(rows, columns_t[:, cols], preferred_element_type=jnp.float32)

    def weigh(index, slot):
        row_part = row_lse[pl.ds(pl.multiple_of(index * block, block), block), :]
        for start in range(0, across, 128):
            cols = slice(start, start + 128)
            scaled = SCALE * scores[slot][:, cols]
            value = jnp.exp2(scaled - row_part) + jnp.exp2(scaled - col_ref[0:1, cols])
            weights[slot][:, cols] = value.astype(jnp.bfloat16)

    def collect(index, slot):
        value = jnp.dot(weights[slot][...], columns[...], preferred_element_type=jnp.float32)
        if not pack:
            half = count // 2
            at = pl.multiple_of(jnp.minimum(index, half) * block, block)
            other_ref[pl.ds(at, block), :] = value.astype(other_ref.dtype)
            at = pl.multiple_of(jnp.maximum(index - half, 0) * block, block)
            own_ref[pl.ds(at, block), :] = value
            return
        for part in range(block // unit):
            place = index * (block // unit) + part
            mine = place == index_ref[0]
            at = pl.multiple_of(place * (unit + TAIL), TAIL)
            piece = value[part * unit : (part + 1) * unit, :]
            out_ref[pl.ds(at, unit), :] = jnp.where(mine, 0.0, piece).astype(out_ref.dtype)
            out_ref[pl.ds(pl.multiple_of(at + unit, TAIL), TAIL), :] = tail[...]
            own_ref[...] = jnp.where(mine, piece, own_ref[...])

    multiply(0, 0)
    multiply(1, 1)
    weigh(0, 0)

    @pl.loop(0, count // 2 - 1)
    def _(turn):
        multiply(2 * turn + 2, 0)
        collect(2 * turn, 0)
        weigh(2 * turn + 1, 1)
        multiply(2 * turn + 3, 1)
        collect(2 * turn + 1, 1)
        weigh(2 * turn + 2, 0)

    collect(count - 2, 0)
    weigh(count - 1, 1)
    collect(count - 1, 1)


def gradient_scratch(total, across, width, block):
    return [
        pltpu.VMEM((width, across), jnp.bfloat16),
        pltpu.VMEM((across, width), jnp.bfloat16),
        [pltpu.VMEM((block, across), jnp.float32)] * 2,
        [pltpu.VMEM((block, across), jnp.bfloat16)] * 2,
        pltpu.VMEM((total, 128), jnp.float32),
        pltpu.VMEM((TAIL, width), jnp.bfloat16),
    ]


def text_gradient(text, own, other, col_parts, row_parts, unit, index):
    total, width = text.shape
    across = 2 * own.shape[0]
    vmem = pl.BlockSpec(memory_space=pltpu.VMEM)
    return pl.pallas_call(
        functools.partial(gradient_kernel, unit, True),
        in_specs=[pl.BlockSpec(memory_space=pltpu.SMEM)] + [vmem] * 5,
        out_shape=[
            jax.ShapeDtypeStruct((total // unit * (unit + TAIL), width), jnp.bfloat16),
            jax.ShapeDtypeStruct((unit, width), jnp.float32),
            jax.ShapeDtypeStruct((8, total), jnp.float32),
            jax.ShapeDtypeStruct((8, across), jnp.float32),
        ],
        scratch_shapes=gradient_scratch(total, across, width, TEXT_BLOCKS * unit),
        compiler_params=pltpu.CompilerParams(vmem_limit_bytes=VMEM_LIMIT),
        cost_estimate=pl.CostEstimate(
            flops=4 * total * across * width, bytes_accessed=4 * (total + across) * width, transcendentals=0
        ),
    )(index, col_parts, row_parts, text, own, other)


def image_gradient(own, other, text, row_lse, col_lse, unit):
    half, width = own.shape
    across = text.shape[0]
    block = IMAGE_BLOCKS * unit
    return pl.pallas_call(
        functools.partial(gradient_kernel, unit, False),
        out_shape=[
            jax.ShapeDtypeStruct((half, width), jnp.float32),
            jax.ShapeDtypeStruct((half + block, width), jnp.bfloat16),
        ],
        scratch_shapes=[pltpu.VMEM((2 * half, width), jnp.bfloat16)] + gradient_scratch(2 * half, across, width, block),
        compiler_params=pltpu.CompilerParams(vmem_limit_bytes=VMEM_LIMIT),
        cost_estimate=pl.CostEstimate(
            flops=0, bytes_accessed=0, transcendentals=0
        ),
    )(row_lse, col_lse, own, other, text)


def pack_kernel(index_ref, term_ref, own_ref, *refs):
    *back_refs, out_ref, mine_ref = refs
    unit = mine_ref.shape[0]
    size = back_refs[0].shape[0]
    tail = tail_of(term_ref[0], out_ref.shape[1])
    for place in range(own_ref.shape[0] // unit):
        part = slice(place * unit, (place + 1) * unit)
        mine = index_ref[0] == place
        start = place * unit % size
        back = back_refs[place * unit // size][start : start + unit, :]
        value = own_ref[part, :] + back.astype(jnp.float32)
        at = place * (unit + TAIL)
        out_ref[at : at + unit, :] = jnp.where(mine, 0.0, value).astype(out_ref.dtype)
        out_ref[at + unit : at + unit + TAIL, :] = tail

        @pl.when(mine)
        def _():
            mine_ref[...] = value


def packed(own, back, unit, index, term):
    total, width = own.shape
    smem = pl.BlockSpec(memory_space=pltpu.SMEM)
    vmem = pl.BlockSpec(memory_space=pltpu.VMEM)
    return pl.pallas_call(
        pack_kernel,
        in_specs=[smem, smem] + [vmem] * (1 + len(back)),
        out_shape=[
            jax.ShapeDtypeStruct((total // unit * (unit + TAIL), width), jnp.bfloat16),
            jax.ShapeDtypeStruct((unit, width), jnp.float32),
        ],
        compiler_params=pltpu.CompilerParams(vmem_limit_bytes=VMEM_LIMIT),
        cost_estimate=pl.CostEstimate(flops=0, bytes_accessed=0, transcendentals=0),
    )(index, term.reshape(1), own, *back)


def finish_kernel(parts_ref, own_ref, pair_ref, grad_ref, scalar_ref):
    count = parts_ref.shape[0]
    rows = own_ref.shape[0]
    value = own_ref[...] - pair_ref[...].astype(jnp.float32)
    tail = jnp.zeros((TAIL, own_ref.shape[1]), jnp.float32)
    for part in range(count):
        value = value + parts_ref[part, :rows, :].astype(jnp.float32)
        tail = tail + parts_ref[part, rows:, :].astype(jnp.float32)
    grad_ref[...] = 100.0 * value
    scalar_ref[...] = tail


def finished(parts, own, pair):
    return pl.pallas_call(
        finish_kernel,
        out_shape=[
            jax.ShapeDtypeStruct(own.shape, jnp.float32),
            jax.ShapeDtypeStruct((TAIL, own.shape[1]), jnp.float32),
        ],
        compiler_params=pltpu.CompilerParams(vmem_limit_bytes=VMEM_LIMIT),
    )(parts, own, pair)


def bits_of(x, y, z):
    return {axis + kind: PAIRS[at][k] for axis, at in zip("xyz", (x, y, z)) for k, kind in enumerate("pq")}


def groups_of(names):
    found = {}
    for z, y, x, core in itertools.product(range(4), range(4), range(4), range(2)):
        bits = bits_of(x, y, z)
        key = tuple(bits[name] for name in sorted(bits) if name not in names) + (core,)
        place = functools.reduce(lambda total, name: 2 * total + bits[name], names, 0)
        found.setdefault(key, {})[place] = ((((z // 2) * 4 + y) * 4 + x) * 2 + z % 2) * 2 + core
    return [[group[place] for place in sorted(group)] for group in found.values()]


def own_bits():
    where = {"x": lax.axis_index("x"), "y": lax.axis_index("y"), "z": 2 * lax.axis_index("zh") + lax.axis_index("zl")}
    bits = {}
    for axis, at in where.items():
        bits[axis + "p"] = jnp.where((at == 1) | (at == 2), 1, 0)
        bits[axis + "q"] = at // 2
    return bits


def place_of(names, bits):
    return functools.reduce(lambda total, name: 2 * total + bits[name], names, 0)


def doubled(value, names, name, bits):
    mask = 1 << (len(names) - 1 - names.index(name))
    pairs = [(group[at], group[at ^ mask]) for group in groups_of(names) for at in range(len(group))]
    back = lax.ppermute(value, AXES, pairs)
    at = lax.broadcasted_iota(jnp.int32, (2,) + (1,) * value.ndim, 0)
    return jnp.where(at == bits[name], value[None], back[None])


def gathered(image, text, bits):
    half = image.shape[0] // 2
    pieces = [image[:half], image[half:], text[:half], text[half:]]
    names = [A_BITS, A_BITS, B_BITS, B_BITS]
    for turn in range(3):
        pieces = [
            doubled(piece, name, name[2 - turn] if k % 2 == 0 else name[2 - (2, 0, 1)[turn]], bits)
            for k, (piece, name) in enumerate(zip(pieces, names))
        ]
    whole = []
    for k in (0, 2):
        both = jnp.stack([pieces[k], jnp.transpose(pieces[k + 1], (2, 0, 1, 3, 4))], axis=3)
        whole.append(both.reshape(16 * half, image.shape[1]))
    return lax.optimization_barrier(tuple(whole))


def swap(value):
    return lax.ppermute(value, "c", [(0, 1), (1, 0)])


def exchanged(blocks, names):
    return lax.all_to_all(
        blocks, AXES, split_axis=0, concat_axis=0, tiled=True, axis_index_groups=groups_of(names)
    )


def joined(first, second):
    peak = jnp.maximum(first, second)
    return peak + jnp.log2(jnp.exp2(first - peak) + jnp.exp2(second - peak))


def body(image_embed, text_embed):
    rows, width = image_embed.shape
    bits = own_bits()
    members = 2 ** len(A_BITS)
    half = members * rows
    batch = rows * 2 * members * members
    at_a = jnp.full((1,), place_of(A_BITS, bits), jnp.int32)
    at_b = jnp.full((1,), place_of(B_BITS, bits), jnp.int32)

    own, text = gathered(image_embed, text_embed, bits)
    other = swap(own)
    row_part, col_parts = forward(own, other, text, image_embed, text_embed, members)

    col_parts = exchanged(col_parts, B_BITS)
    row_part = row_part.reshape(2, half // 128, 128)
    row_part = joined(row_part, swap(row_part)[::-1]).reshape(1, 2 * half // 128, 128)
    row_parts = exchanged(jnp.broadcast_to(row_part, (members,) + row_part.shape[1:]), A_BITS)

    text_sum, text_own, col_lse, row_lse = text_gradient(text, own, other, col_parts, row_parts, rows, at_b)
    term_c = LN2 * jnp.sum(col_lse[0] - 1.0) - 2.0 * jnp.sum(col_parts[:, -1, 0])
    text_sum, own, other = lax.optimization_barrier((text_sum, own, other))
    text_parts = exchanged(text_sum.reshape(members, rows + TAIL, width), B_BITS)
    image_half, image_other = image_gradient(own, other, text, row_lse, col_lse, rows)
    quarter = half // 4
    image_back = [swap(image_other[k * quarter : (k + 1) * quarter]) for k in range(4)]
    term_a = term_c + swap(jnp.full((8, 128), term_c))[0, 0]
    image_sum, image_own = packed(image_half, image_back, rows, at_a, term_a)
    image_parts = exchanged(image_sum.reshape(members, rows + TAIL, width), A_BITS)
    text_grad, tail_b = finished(text_parts, text_own, image_embed)
    image_grad, tail_a = finished(image_parts, image_own, text_embed)
    mean_loss = (jnp.sum(tail_a[0, :3]) + jnp.sum(tail_b[0, :3])) / (2.0 * batch)
    return (image_grad, text_grad, mean_loss.reshape(1))


def solution(mesh):
    fine = Mesh(mesh.devices.reshape(2, 4, 4, 2, 2), AXES)
    spec = P(AXES, None)
    return jax.shard_map(body, mesh=fine, in_specs=(spec, spec), out_specs=(spec, spec, P()), check_vma=False)
```

```python
import functools
import itertools
import math

import jax
import jax.numpy as jnp
from jax import lax
from jax.experimental import pallas as pl
from jax.experimental.pallas import tpu as pltpu
from jax.sharding import Mesh, PartitionSpec as P

AXES = ("zh", "y", "x", "zl", "c")
A_BITS = ("zp", "yq", "yp")
B_BITS = ("zq", "xq", "xp")
PAIRS = ((0, 0), (1, 0), (1, 1), (0, 1))
SWAP = [(0, 1), (1, 0)]
LOG2E = math.log2(math.e)
LN2 = math.log(2.0)
SCALE = 100.0 * LOG2E
BLOCK = 256
TAIL = 16
TEXT_BLOCKS = 1
PARTS = 4
VMEM_LIMIT = 56 * 1024 * 1024


def forward_kernel(own_ref, other_ref, text_ref, image_ref, pair_ref, row_ref, col_ref, text_t, image, scores, block_max, row_max, row_sum, col_max, col_sum):
    half = own_ref.shape[0]
    columns = text_ref.shape[0]
    count = 2 * half // BLOCK
    text_t[...] = text_ref[...].T
    image[:half, :] = own_ref[...]
    image[half:, :] = other_ref[...]
    col_max[...] = jnp.full(col_max.shape, -1e30, jnp.float32)
    col_sum[...] = jnp.zeros(col_sum.shape, jnp.float32)

    def multiply(index, slot):
        at = pl.multiple_of(jnp.minimum(index, count - 1) * BLOCK, BLOCK)
        rows = image[pl.ds(at, BLOCK), :]
        for start in range(0, columns, BLOCK):
            cols = slice(start, start + BLOCK)
            part = SCALE * jnp.dot(rows, text_t[:, cols], preferred_element_type=jnp.float32)
            scores[slot][:, cols] = part
            block_max[slot][:, cols] = jnp.max(part.reshape(BLOCK // 8, 8, BLOCK), axis=0)

    def sums(index, slot):
        old = col_max[...]
        peak = jnp.maximum(old, block_max[slot][...])
        col_max[...] = peak
        total = col_sum[...] * jnp.exp2(old - peak)
        for start in range(0, BLOCK, 8):
            block = scores[slot][start : start + 8, :]
            pieces = [block[:, k : k + 128] for k in range(0, columns, 128)]
            top = functools.reduce(jnp.maximum, pieces)
            at = pl.multiple_of(index * BLOCK + start, 8)
            row_max[pl.ds(at, 8), :] = top
            row_sum[pl.ds(at, 8), :] = functools.reduce(jnp.add, [jnp.exp2(piece - top) for piece in pieces])
            total = total + jnp.exp2(block - peak)
        col_sum[...] = total

    multiply(0, 0)

    @pl.loop(0, count // 2)
    def _(turn):
        multiply(2 * turn + 1, 1)
        sums(2 * turn, 0)
        multiply(2 * turn + 2, 0)
        sums(2 * turn + 1, 1)

    tops = row_max[...].T
    parts = row_sum[...].T
    peak = jnp.max(tops, axis=0, keepdims=True)
    total = jnp.sum(parts * jnp.exp2(tops - peak), axis=0, keepdims=True)
    row_lse = peak + jnp.log2(total)
    for k in range(2 * half // 128):
        row_ref[k : k + 1, :] = row_lse[:, k * 128 : k * 128 + 128]
    peak = jnp.max(col_max[...], axis=0, keepdims=True)
    total = jnp.sum(col_sum[...] * jnp.exp2(col_max[...] - peak), axis=0, keepdims=True)
    col_lse = peak + jnp.log2(total)
    products = image_ref[...].astype(jnp.float32) * pair_ref[...].astype(jnp.float32)
    diagonal = 100.0 * jnp.sum(jnp.sum(products, axis=0, keepdims=True), axis=1, keepdims=True)
    count = columns // 128
    for place in range(col_ref.shape[0]):
        for k in range(count):
            col_ref[place, k : k + 1, :] = col_lse[:, k * 128 : k * 128 + 128]
        col_ref[place, count:, :] = jnp.broadcast_to(diagonal, (col_ref.shape[1] - count, 128))


def forward(own, other, text, image, pair, members):
    half, width = own.shape
    columns = text.shape[0]
    elements = 2 * half * columns
    f32 = lambda *shape: pltpu.VMEM(shape, jnp.float32)
    return pl.pallas_call(
        forward_kernel,
        out_shape=[
            jax.ShapeDtypeStruct((2 * half // 128, 128), jnp.float32),
            jax.ShapeDtypeStruct((members, columns // 128 + 2, 128), jnp.float32),
        ],
        scratch_shapes=[
            pltpu.VMEM((width, columns), jnp.bfloat16),
            pltpu.VMEM((2 * half, width), jnp.bfloat16),
            [f32(BLOCK, columns), f32(BLOCK, columns)],
            [f32(8, columns), f32(8, columns)],
            f32(2 * half, 128),
            f32(2 * half, 128),
            f32(8, columns),
            f32(8, columns),
        ],
        compiler_params=pltpu.CompilerParams(vmem_limit_bytes=VMEM_LIMIT),
        cost_estimate=pl.CostEstimate(
            flops=2 * elements * width, bytes_accessed=4 * (half + columns) * width, transcendentals=2 * elements
        ),
    )(own, other, text, image, pair)


def tail_of(scalar, width):
    spread = jnp.broadcast_to(scalar, (TAIL, width))
    high = spread.astype(jnp.bfloat16).astype(jnp.float32)
    middle = (spread - high).astype(jnp.bfloat16).astype(jnp.float32)
    low = spread - high - middle
    lane = lax.broadcasted_iota(jnp.int32, (TAIL, width), 1)
    values = jnp.where(lane == 0, high, jnp.where(lane == 1, middle, jnp.where(lane == 2, low, 0.0)))
    return values.astype(jnp.bfloat16)


def whole_lse(parts_ref, lse_ref):
    count = lse_ref.shape[1] // 128
    parts = parts_ref[:, :count, :]
    peak = jnp.max(parts, axis=0)
    value = peak + jnp.log2(jnp.sum(jnp.exp2(parts - peak[None]), axis=0)) + 1.0
    for k in range(count):
        lse_ref[:, k * 128 : k * 128 + 128] = jnp.broadcast_to(value[k : k + 1, :], (8, 128))


def gradient_kernel(unit, pack, *refs):
    if pack:
        index_ref, row_parts, col_parts, rows_ref, first_ref, second_ref, *refs = refs
        out_ref, own_ref, row_ref, col_ref, term_ref, *refs = refs
        whole_lse(row_parts, row_ref)
        whole_lse(col_parts, col_ref)
        lse_sum = jnp.sum(row_ref[0:1, :] - 1.0, axis=1, keepdims=True)
        diagonal = jnp.sum(row_parts[:, row_parts.shape[1] - 1, 0:1], axis=0, keepdims=True)
        term_ref[...] = jnp.broadcast_to(LN2 * lse_sum - 2.0 * diagonal, term_ref.shape)
        column_refs = (first_ref, second_ref)
    else:
        index_ref, row_ref, col_ref, own_rows, other_rows, column_ref, *refs = refs
        mine_ref, out_ref, *refs = refs
        other_refs, (rows_ref, *refs) = refs[:PARTS], refs[PARTS:]
        rows_ref[: other_rows.shape[0], :] = other_rows[...]
        rows_ref[other_rows.shape[0] :, :] = own_rows[...]
        column_refs = (column_ref,)
    columns_t, columns, scores, weights, row_lse, tail = refs
    total = rows_ref.shape[0]
    block = weights[0].shape[0]
    count = total // block
    size = column_refs[0].shape[0]
    for piece, column_ref in enumerate(column_refs):
        part = slice(piece * size, (piece + 1) * size)
        columns_t[:, part] = column_ref[...].T
        columns[part, :] = column_ref[...]
    across = columns.shape[0]
    if pack:
        row_lse[...] = jnp.broadcast_to(row_ref[0:1, :], (128, total)).T
        halves = [col_ref[0:1, : across // 2], col_ref[0:1, across // 2 :]]
        sums = [jnp.sum(half - 1.0, axis=1, keepdims=True) for half in halves]
        tail[...] = tail_of(LN2 * (sums[0] + sums[1]), tail.shape[1])
    else:
        row_lse[: total // 2, :] = jnp.broadcast_to(row_ref[0:1, total // 2 :], (128, total // 2)).T
        row_lse[total // 2 :, :] = jnp.broadcast_to(row_ref[0:1, : total // 2], (128, total // 2)).T

    def rows_at(index):
        if isinstance(index, int):
            return slice(index * block, (index + 1) * block)
        return pl.ds(pl.multiple_of(index * block, block), block)

    def multiply(index, slot):
        rows = rows_ref[rows_at(index), :]
        for start in range(0, across, BLOCK):
            cols = slice(start, start + BLOCK)
            scores[slot][:, cols] = jnp.dot(rows, columns_t[:, cols], preferred_element_type=jnp.float32)

    def weigh(index, slot):
        row_part = row_lse[rows_at(index), :]
        for start in range(0, across, 128):
            cols = slice(start, start + 128)
            scaled = SCALE * scores[slot][:, cols]
            value = jnp.exp2(scaled - row_part) + jnp.exp2(scaled - col_ref[0:1, cols])
            weights[slot][:, cols] = value.astype(jnp.bfloat16)

    def collect(index, slot):
        value = jnp.dot(weights[slot][...], columns[...], preferred_element_type=jnp.float32)
        if not pack:
            if index < PARTS:
                other_refs[index][...] = value.astype(out_ref.dtype)
                return
            out_ref[(index - PARTS) * block : (index - PARTS + 1) * block, :] = value.astype(out_ref.dtype)
            for part in range(block // unit):
                mine = (index - PARTS) * (block // unit) + part == index_ref[0]
                mine_ref[...] = jnp.where(mine, value[part * unit : (part + 1) * unit, :], mine_ref[...])
            return
        for part in range(block // unit):
            place = index * (block // unit) + part
            mine = place == index_ref[0]
            at = pl.multiple_of(place * (unit + TAIL), TAIL)
            piece = value[part * unit : (part + 1) * unit, :]
            out_ref[pl.ds(at, unit), :] = jnp.where(mine, 0.0, piece).astype(out_ref.dtype)
            out_ref[pl.ds(pl.multiple_of(at + unit, TAIL), TAIL), :] = tail[...]
            own_ref[...] = jnp.where(mine, piece, own_ref[...])

    multiply(0, 0)
    multiply(1, 1)
    weigh(0, 0)

    def turns(turn):
        multiply(2 * turn + 2, 0)
        collect(2 * turn, 0)
        weigh(2 * turn + 1, 1)
        multiply(2 * turn + 3, 1)
        collect(2 * turn + 1, 1)
        weigh(2 * turn + 2, 0)

    if pack:
        pl.loop(0, count // 2 - 1)(turns)
    else:
        for turn in range(count // 2 - 1):
            turns(turn)
    collect(count - 2, 0)
    weigh(count - 1, 1)
    collect(count - 1, 1)


def gradient_scratch(total, across, width, block):
    return [
        pltpu.VMEM((width, across), jnp.bfloat16),
        pltpu.VMEM((across, width), jnp.bfloat16),
        [pltpu.VMEM((block, across), jnp.float32)] * 2,
        [pltpu.VMEM((block, across), jnp.bfloat16)] * 2,
        pltpu.VMEM((total, 128), jnp.float32),
        pltpu.VMEM((TAIL, width), jnp.bfloat16),
    ]


def text_gradient(text, own, other, col_parts, row_parts, unit, index):
    total, width = text.shape
    across = 2 * own.shape[0]
    vmem = pl.BlockSpec(memory_space=pltpu.VMEM)
    return pl.pallas_call(
        functools.partial(gradient_kernel, unit, True),
        in_specs=[pl.BlockSpec(memory_space=pltpu.SMEM)] + [vmem] * 5,
        out_shape=[
            jax.ShapeDtypeStruct((total // unit * (unit + TAIL), width), jnp.bfloat16),
            jax.ShapeDtypeStruct((unit, width), jnp.float32),
            jax.ShapeDtypeStruct((8, total), jnp.float32),
            jax.ShapeDtypeStruct((8, across), jnp.float32),
            jax.ShapeDtypeStruct((8, 128), jnp.float32),
        ],
        scratch_shapes=gradient_scratch(total, across, width, TEXT_BLOCKS * unit),
        compiler_params=pltpu.CompilerParams(vmem_limit_bytes=VMEM_LIMIT),
        cost_estimate=pl.CostEstimate(
            flops=4 * total * across * width, bytes_accessed=4 * (total + across) * width, transcendentals=0
        ),
    )(index, col_parts, row_parts, text, own, other)


def image_gradient(own, other, text, row_lse, col_lse, unit, index):
    half, width = own.shape
    across = text.shape[0]
    block = half // PARTS
    return pl.pallas_call(
        functools.partial(gradient_kernel, unit, False),
        in_specs=[pl.BlockSpec(memory_space=pltpu.SMEM)] + [pl.BlockSpec(memory_space=pltpu.VMEM)] * 5,
        out_shape=[
            jax.ShapeDtypeStruct((unit, width), jnp.float32),
            jax.ShapeDtypeStruct((half, width), jnp.bfloat16),
        ]
        + [jax.ShapeDtypeStruct((block, width), jnp.bfloat16)] * PARTS,
        scratch_shapes=[pltpu.VMEM((2 * half, width), jnp.bfloat16)] + gradient_scratch(2 * half, across, width, block),
        compiler_params=pltpu.CompilerParams(vmem_limit_bytes=VMEM_LIMIT),
        cost_estimate=pl.CostEstimate(
            flops=0, bytes_accessed=0, transcendentals=0
        ),
    )(index, row_lse, col_lse, own, other, text)


def pack_kernel(index_ref, term_ref, term_back_ref, part_ref, own_ref, *refs):
    *back_refs, out_ref, mine_ref = refs
    unit = mine_ref.shape[0]
    size = back_refs[0].shape[0]
    tail = tail_of(term_ref[0:1, 0:1] + term_back_ref[0:1, 0:1], out_ref.shape[1])
    for place in range(own_ref.shape[0] // unit):
        part = slice(place * unit, (place + 1) * unit)
        mine = index_ref[0] == place
        start = place * unit % size
        back = back_refs[place * unit // size][start : start + unit, :]
        back = back.astype(jnp.float32)
        value = own_ref[part, :].astype(jnp.float32) + back
        at = place * (unit + TAIL)
        out_ref[at : at + unit, :] = jnp.where(mine, 0.0, value).astype(out_ref.dtype)
        out_ref[at + unit : at + unit + TAIL, :] = tail

        @pl.when(mine)
        def _():
            mine_ref[...] = part_ref[...] + back


def packed(part, own, back, unit, index, terms):
    total, width = own.shape
    smem = pl.BlockSpec(memory_space=pltpu.SMEM)
    vmem = pl.BlockSpec(memory_space=pltpu.VMEM)
    return pl.pallas_call(
        pack_kernel,
        in_specs=[smem] + [vmem] * (4 + len(back)),
        out_shape=[
            jax.ShapeDtypeStruct((total // unit * (unit + TAIL), width), jnp.bfloat16),
            jax.ShapeDtypeStruct((unit, width), jnp.float32),
        ],
        compiler_params=pltpu.CompilerParams(vmem_limit_bytes=VMEM_LIMIT),
        cost_estimate=pl.CostEstimate(flops=0, bytes_accessed=0, transcendentals=0),
    )(index, *terms, part, own, *back)


def finish_kernel(divisor, parts_ref, own_ref, pair_ref, *refs):
    if divisor is None:
        grad_ref, scalar_ref = refs
    else:
        other_ref, grad_ref, loss_ref = refs
    count = parts_ref.shape[0]
    rows = own_ref.shape[0]
    value = own_ref[...] - pair_ref[...].astype(jnp.float32)
    tail = jnp.zeros((TAIL, own_ref.shape[1]), jnp.float32)
    for part in range(count):
        value = value + parts_ref[part, :rows, :].astype(jnp.float32)
        tail = tail + parts_ref[part, rows:, :].astype(jnp.float32)
    grad_ref[...] = 100.0 * value
    if divisor is None:
        scalar_ref[...] = tail
    else:
        loss_ref[0] = jnp.sum(tail[0:1, :] + other_ref[0:1, :]) / divisor


def finished(parts, own, pair, scalars=None, divisor=None):
    vmem = pl.BlockSpec(memory_space=pltpu.VMEM)
    if divisor is None:
        last, place, given = jax.ShapeDtypeStruct((TAIL, own.shape[1]), jnp.float32), vmem, []
    else:
        last, place, given = jax.ShapeDtypeStruct((1,), jnp.float32), pl.BlockSpec(memory_space=pltpu.SMEM), [scalars]
    return pl.pallas_call(
        functools.partial(finish_kernel, divisor),
        in_specs=[vmem] * (3 + len(given)),
        out_specs=[vmem, place],
        out_shape=[jax.ShapeDtypeStruct(own.shape, jnp.float32), last],
        compiler_params=pltpu.CompilerParams(vmem_limit_bytes=VMEM_LIMIT),
    )(parts, own, pair, *given)


def bits_of(x, y, z):
    return {axis + kind: PAIRS[at][k] for axis, at in zip("xyz", (x, y, z)) for k, kind in enumerate("pq")}


def groups_of(names):
    found = {}
    for z, y, x, core in itertools.product(range(4), range(4), range(4), range(2)):
        bits = bits_of(x, y, z)
        key = tuple(bits[name] for name in sorted(bits) if name not in names) + (core,)
        place = functools.reduce(lambda total, name: 2 * total + bits[name], names, 0)
        found.setdefault(key, {})[place] = ((((z // 2) * 4 + y) * 4 + x) * 2 + z % 2) * 2 + core
    return [[group[place] for place in sorted(group)] for group in found.values()]


def own_bits():
    where = {"x": lax.axis_index("x"), "y": lax.axis_index("y"), "z": 2 * lax.axis_index("zh") + lax.axis_index("zl")}
    bits = {}
    for axis, at in where.items():
        bits[axis + "p"] = jnp.where((at == 1) | (at == 2), 1, 0)
        bits[axis + "q"] = at // 2
    return bits


def place_of(names, bits):
    return functools.reduce(lambda total, name: 2 * total + bits[name], names, 0)


def doubled(value, names, name, bits):
    mask = 1 << (len(names) - 1 - names.index(name))
    pairs = [(group[at], group[at ^ mask]) for group in groups_of(names) for at in range(len(group))]
    back = lax.ppermute(value, AXES, pairs)
    at = lax.broadcasted_iota(jnp.int32, (2,) + (1,) * value.ndim, 0)
    return jnp.where(at == bits[name], value[None], back[None])


def gathered(image, text, bits):
    half = image.shape[0] // 2
    pieces = [image[:half], image[half:], text[:half], text[half:]]
    names = [A_BITS, A_BITS, B_BITS, B_BITS]
    for turn in range(3):
        pieces = [
            doubled(piece, name, name[2 - turn] if k % 2 == 0 else name[2 - (2, 0, 1)[turn]], bits)
            for k, (piece, name) in enumerate(zip(pieces, names))
        ]
    whole = []
    for k in (0, 2):
        both = jnp.stack([pieces[k], jnp.transpose(pieces[k + 1], (2, 0, 1, 3, 4))], axis=3)
        whole.append(both.reshape(16 * half, image.shape[1]))
    return lax.optimization_barrier(tuple(whole))


def swap(value):
    return lax.ppermute(value, "c", [(0, 1), (1, 0)])


def exchanged(blocks, names):
    return lax.all_to_all(
        blocks, AXES, split_axis=0, concat_axis=0, tiled=True, axis_index_groups=groups_of(names)
    )


def joined(first, second):
    peak = jnp.maximum(first, second)
    return peak + jnp.log2(jnp.exp2(first - peak) + jnp.exp2(second - peak))


def body(image_embed, text_embed):
    rows, width = image_embed.shape
    bits = own_bits()
    members = 2 ** len(A_BITS)
    half = members * rows
    batch = rows * 2 * members * members
    at_a = jnp.full((1,), place_of(A_BITS, bits), jnp.int32)
    at_b = jnp.full((1,), place_of(B_BITS, bits), jnp.int32)

    own, text = gathered(image_embed, text_embed, bits)
    other = swap(own)
    row_part, col_parts = forward(own, other, text, image_embed, text_embed, members)

    col_parts = exchanged(col_parts, B_BITS)
    count = half // 128
    back = swap(row_part)
    row_part = joined(row_part, jnp.concatenate([back[count:], back[:count]], axis=0))
    row_parts = exchanged(jnp.broadcast_to(row_part[None], (members,) + row_part.shape), A_BITS)

    text_sum, text_own, col_lse, row_lse, term = text_gradient(text, own, other, col_parts, row_parts, rows, at_b)
    term_back = swap(term)
    text_sum, own, other = lax.optimization_barrier((text_sum, own, other))
    text_parts = exchanged(text_sum.reshape(members, rows + TAIL, width), B_BITS)
    image_mine, image_half, *image_other = image_gradient(own, other, text, row_lse, col_lse, rows, at_a)
    image_back = [swap(piece) for piece in image_other]
    image_sum, image_own = packed(image_mine, image_half, image_back, rows, at_a, (term, term_back))
    image_parts = exchanged(image_sum.reshape(members, rows + TAIL, width), A_BITS)
    text_grad, tail_b = finished(text_parts, text_own, image_embed)
    image_grad, mean_loss = finished(image_parts, image_own, text_embed, tail_b, 2.0 * batch)
    return (image_grad, text_grad, mean_loss)


def solution(mesh):
    fine = Mesh(mesh.devices.reshape(2, 4, 4, 2, 2), AXES)
    spec = P(AXES, None)
    return jax.shard_map(body, mesh=fine, in_specs=(spec, spec), out_specs=(spec, spec, P()), check_vma=False)
```

```python
import functools
import itertools
import math

import jax
import jax.numpy as jnp
from jax import lax
from jax.experimental import pallas as pl
from jax.experimental.pallas import tpu as pltpu
from jax.sharding import Mesh, PartitionSpec as P

AXES = ("zh", "y", "x", "zl", "c")
A_BITS = ("zp", "yq", "yp")
B_BITS = ("zq", "xq", "xp")
PAIRS = ((0, 0), (1, 0), (1, 1), (0, 1))
SWAP = [(0, 1), (1, 0)]
LOG2E = math.log2(math.e)
LN2 = math.log(2.0)
SCALE = 100.0 * LOG2E
BLOCK = 256
TAIL = 16
TEXT_BLOCKS = 1
PARTS = 4
VMEM_LIMIT = 56 * 1024 * 1024


def forward_kernel(own_ref, other_ref, text_ref, image_ref, pair_ref, row_ref, col_ref, text_t, scores, block_max, col_max, col_sum):
    half = own_ref.shape[0]
    columns = text_ref.shape[0]
    count = 2 * half // BLOCK
    text_t[...] = text_ref[...].T
    col_max[...] = jnp.full(col_max.shape, -1e30, jnp.float32)
    col_sum[...] = jnp.zeros(col_sum.shape, jnp.float32)

    def multiply(index, slot):
        piece, at = (own_ref, index * BLOCK) if index * BLOCK < half else (other_ref, index * BLOCK - half)
        rows = piece[at : at + BLOCK, :]
        for start in range(0, columns, BLOCK):
            cols = slice(start, start + BLOCK)
            part = SCALE * jnp.dot(rows, text_t[:, cols], preferred_element_type=jnp.float32)
            scores[slot][:, cols] = part
            block_max[slot][:, cols] = jnp.max(part.reshape(BLOCK // 8, 8, BLOCK), axis=0)

    def sums(index, slot):
        old = col_max[...]
        peak = jnp.maximum(old, block_max[slot][...])
        col_max[...] = peak
        total = col_sum[...] * jnp.exp2(old - peak)
        tops, parts = [], []
        for start in range(0, BLOCK, 8):
            block = scores[slot][start : start + 8, :]
            pieces = [block[:, k : k + 128] for k in range(0, columns, 128)]
            top = functools.reduce(jnp.maximum, pieces)
            tops.append(top)
            parts.append(functools.reduce(jnp.add, [jnp.exp2(piece - top) for piece in pieces]))
            total = total + jnp.exp2(block - peak)
        col_sum[...] = total
        tops = jnp.concatenate(tops, axis=0).T
        parts = jnp.concatenate(parts, axis=0).T
        top = jnp.max(tops, axis=0, keepdims=True)
        row_lse = top + jnp.log2(jnp.sum(parts * jnp.exp2(tops - top), axis=0, keepdims=True))
        for k in range(BLOCK // 128):
            at = index * (BLOCK // 128) + k
            row_ref[at : at + 1, :] = row_lse[:, k * 128 : k * 128 + 128]

    multiply(0, 0)

    for index in range(count):
        if index + 1 < count:
            multiply(index + 1, (index + 1) % 2)
        sums(index, index % 2)

    peak = jnp.max(col_max[...], axis=0, keepdims=True)
    total = jnp.sum(col_sum[...] * jnp.exp2(col_max[...] - peak), axis=0, keepdims=True)
    col_lse = peak + jnp.log2(total)
    products = image_ref[...].astype(jnp.float32) * pair_ref[...].astype(jnp.float32)
    diagonal = 100.0 * jnp.sum(jnp.sum(products, axis=0, keepdims=True), axis=1, keepdims=True)
    count = columns // 128
    for place in range(col_ref.shape[0]):
        for k in range(count):
            col_ref[place, k : k + 1, :] = col_lse[:, k * 128 : k * 128 + 128]
        col_ref[place, count:, :] = jnp.broadcast_to(diagonal, (col_ref.shape[1] - count, 128))


def forward(own, other, text, image, pair, members):
    half, width = own.shape
    columns = text.shape[0]
    elements = 2 * half * columns
    f32 = lambda *shape: pltpu.VMEM(shape, jnp.float32)
    return pl.pallas_call(
        forward_kernel,
        out_shape=[
            jax.ShapeDtypeStruct((2 * half // 128, 128), jnp.float32),
            jax.ShapeDtypeStruct((members, columns // 128 + 2, 128), jnp.float32),
        ],
        scratch_shapes=[
            pltpu.VMEM((width, columns), jnp.bfloat16),
            [f32(BLOCK, columns), f32(BLOCK, columns)],
            [f32(8, columns), f32(8, columns)],
            f32(8, columns),
            f32(8, columns),
        ],
        compiler_params=pltpu.CompilerParams(vmem_limit_bytes=VMEM_LIMIT),
        cost_estimate=pl.CostEstimate(
            flops=2 * elements * width, bytes_accessed=4 * (half + columns) * width, transcendentals=2 * elements
        ),
    )(own, other, text, image, pair)


def tail_of(scalar, width):
    spread = jnp.broadcast_to(scalar, (TAIL, width))
    high = spread.astype(jnp.bfloat16).astype(jnp.float32)
    middle = (spread - high).astype(jnp.bfloat16).astype(jnp.float32)
    low = spread - high - middle
    lane = lax.broadcasted_iota(jnp.int32, (TAIL, width), 1)
    values = jnp.where(lane == 0, high, jnp.where(lane == 1, middle, jnp.where(lane == 2, low, 0.0)))
    return values.astype(jnp.bfloat16)


def whole_lse(parts_ref, lse_ref):
    count = lse_ref.shape[1] // 128
    parts = parts_ref[:, :count, :]
    peak = jnp.max(parts, axis=0)
    value = peak + jnp.log2(jnp.sum(jnp.exp2(parts - peak[None]), axis=0)) + 1.0
    for k in range(count):
        lse_ref[:, k * 128 : k * 128 + 128] = jnp.broadcast_to(value[k : k + 1, :], (8, 128))


def gradient_kernel(unit, pack, *refs):
    if pack:
        index_ref, row_parts, col_parts, rows_ref, first_ref, second_ref, *refs = refs
        out_ref, own_ref, row_ref, col_ref, term_ref, *refs = refs
        whole_lse(row_parts, row_ref)
        whole_lse(col_parts, col_ref)
        lse_sum = jnp.sum(row_ref[0:1, :] - 1.0, axis=1, keepdims=True)
        diagonal = jnp.sum(row_parts[:, row_parts.shape[1] - 1, 0:1], axis=0, keepdims=True)
        term_ref[...] = jnp.broadcast_to(LN2 * lse_sum - 2.0 * diagonal, term_ref.shape)
        column_refs = (first_ref, second_ref)
    else:
        index_ref, row_ref, col_ref, own_rows, other_rows, column_ref, *refs = refs
        mine_ref, out_ref, *refs = refs
        other_refs, (rows_ref, *refs) = refs[:PARTS], refs[PARTS:]
        rows_ref[: other_rows.shape[0], :] = other_rows[...]
        rows_ref[other_rows.shape[0] :, :] = own_rows[...]
        column_refs = (column_ref,)
    columns_t, columns, scores, weights, row_lse, tail = refs
    total = rows_ref.shape[0]
    block = weights[0].shape[0]
    count = total // block
    size = column_refs[0].shape[0]
    for piece, column_ref in enumerate(column_refs):
        part = slice(piece * size, (piece + 1) * size)
        columns_t[:, part] = column_ref[...].T
        columns[part, :] = column_ref[...]
    across = columns.shape[0]
    if pack:
        row_lse[...] = jnp.broadcast_to(row_ref[0:1, :], (128, total)).T
        halves = [col_ref[0:1, : across // 2], col_ref[0:1, across // 2 :]]
        sums = [jnp.sum(half - 1.0, axis=1, keepdims=True) for half in halves]
        tail[...] = tail_of(LN2 * (sums[0] + sums[1]), tail.shape[1])
    else:
        row_lse[: total // 2, :] = jnp.broadcast_to(row_ref[0:1, total // 2 :], (128, total // 2)).T
        row_lse[total // 2 :, :] = jnp.broadcast_to(row_ref[0:1, : total // 2], (128, total // 2)).T

    def rows_at(index):
        return slice(index * block, (index + 1) * block)

    def multiply(index, slot):
        rows = rows_ref[rows_at(index), :]
        for start in range(0, across, BLOCK):
            cols = slice(start, start + BLOCK)
            scores[slot][:, cols] = jnp.dot(rows, columns_t[:, cols], preferred_element_type=jnp.float32)

    def weigh(index, slot):
        row_part = row_lse[rows_at(index), :]
        for start in range(0, across, 128):
            cols = slice(start, start + 128)
            scaled = SCALE * scores[slot][:, cols]
            value = jnp.exp2(scaled - row_part) + jnp.exp2(scaled - col_ref[0:1, cols])
            weights[slot][:, cols] = value.astype(jnp.bfloat16)

    def collect(index, slot):
        value = jnp.dot(weights[slot][...], columns[...], preferred_element_type=jnp.float32)
        if not pack:
            if index < PARTS:
                other_refs[index][...] = value.astype(out_ref.dtype)
                return
            out_ref[(index - PARTS) * block : (index - PARTS + 1) * block, :] = value.astype(out_ref.dtype)
            for part in range(block // unit):
                mine = (index - PARTS) * (block // unit) + part == index_ref[0]
                mine_ref[...] = jnp.where(mine, value[part * unit : (part + 1) * unit, :], mine_ref[...])
            return
        for part in range(block // unit):
            place = index * (block // unit) + part
            mine = place == index_ref[0]
            at = place * (unit + TAIL)
            piece = value[part * unit : (part + 1) * unit, :]
            out_ref[at : at + unit, :] = jnp.where(mine, 0.0, piece).astype(out_ref.dtype)
            out_ref[at + unit : at + unit + TAIL, :] = tail[...]
            own_ref[...] = jnp.where(mine, piece, own_ref[...])

    multiply(0, 0)
    multiply(1, 1)
    weigh(0, 0)

    def turns(turn):
        multiply(2 * turn + 2, 0)
        collect(2 * turn, 0)
        weigh(2 * turn + 1, 1)
        multiply(2 * turn + 3, 1)
        collect(2 * turn + 1, 1)
        weigh(2 * turn + 2, 0)

    for turn in range(count // 2 - 1):
        turns(turn)
    collect(count - 2, 0)
    weigh(count - 1, 1)
    collect(count - 1, 1)


def gradient_scratch(total, across, width, block):
    return [
        pltpu.VMEM((width, across), jnp.bfloat16),
        pltpu.VMEM((across, width), jnp.bfloat16),
        [pltpu.VMEM((block, across), jnp.float32)] * 2,
        [pltpu.VMEM((block, across), jnp.bfloat16)] * 2,
        pltpu.VMEM((total, 128), jnp.float32),
        pltpu.VMEM((TAIL, width), jnp.bfloat16),
    ]


def text_gradient(text, own, other, col_parts, row_parts, unit, index):
    total, width = text.shape
    across = 2 * own.shape[0]
    vmem = pl.BlockSpec(memory_space=pltpu.VMEM)
    return pl.pallas_call(
        functools.partial(gradient_kernel, unit, True),
        in_specs=[pl.BlockSpec(memory_space=pltpu.SMEM)] + [vmem] * 5,
        out_shape=[
            jax.ShapeDtypeStruct((total // unit * (unit + TAIL), width), jnp.bfloat16),
            jax.ShapeDtypeStruct((unit, width), jnp.float32),
            jax.ShapeDtypeStruct((8, total), jnp.float32),
            jax.ShapeDtypeStruct((8, across), jnp.float32),
            jax.ShapeDtypeStruct((8, 128), jnp.float32),
        ],
        scratch_shapes=gradient_scratch(total, across, width, TEXT_BLOCKS * unit),
        compiler_params=pltpu.CompilerParams(vmem_limit_bytes=VMEM_LIMIT),
        cost_estimate=pl.CostEstimate(
            flops=4 * total * across * width, bytes_accessed=4 * (total + across) * width, transcendentals=0
        ),
    )(index, col_parts, row_parts, text, own, other)


def image_gradient(own, other, text, row_lse, col_lse, unit, index):
    half, width = own.shape
    across = text.shape[0]
    block = half // PARTS
    return pl.pallas_call(
        functools.partial(gradient_kernel, unit, False),
        in_specs=[pl.BlockSpec(memory_space=pltpu.SMEM)] + [pl.BlockSpec(memory_space=pltpu.VMEM)] * 5,
        out_shape=[
            jax.ShapeDtypeStruct((unit, width), jnp.float32),
            jax.ShapeDtypeStruct((half, width), jnp.bfloat16),
        ]
        + [jax.ShapeDtypeStruct((block, width), jnp.bfloat16)] * PARTS,
        scratch_shapes=[pltpu.VMEM((2 * half, width), jnp.bfloat16)] + gradient_scratch(2 * half, across, width, block),
        compiler_params=pltpu.CompilerParams(vmem_limit_bytes=VMEM_LIMIT),
        cost_estimate=pl.CostEstimate(
            flops=0, bytes_accessed=0, transcendentals=0
        ),
    )(index, row_lse, col_lse, own, other, text)


def pack_kernel(index_ref, term_ref, term_back_ref, part_ref, own_ref, *refs):
    *back_refs, out_ref, mine_ref = refs
    unit = mine_ref.shape[0]
    size = back_refs[0].shape[0]
    tail = tail_of(term_ref[0:1, 0:1] + term_back_ref[0:1, 0:1], out_ref.shape[1])
    for place in range(own_ref.shape[0] // unit):
        part = slice(place * unit, (place + 1) * unit)
        mine = index_ref[0] == place
        start = place * unit % size
        back = back_refs[place * unit // size][start : start + unit, :]
        back = back.astype(jnp.float32)
        value = own_ref[part, :].astype(jnp.float32) + back
        at = place * (unit + TAIL)
        out_ref[at : at + unit, :] = jnp.where(mine, 0.0, value).astype(out_ref.dtype)
        out_ref[at + unit : at + unit + TAIL, :] = tail

        @pl.when(mine)
        def _():
            mine_ref[...] = part_ref[...] + back


def packed(part, own, back, unit, index, terms):
    total, width = own.shape
    smem = pl.BlockSpec(memory_space=pltpu.SMEM)
    vmem = pl.BlockSpec(memory_space=pltpu.VMEM)
    return pl.pallas_call(
        pack_kernel,
        in_specs=[smem] + [vmem] * (4 + len(back)),
        out_shape=[
            jax.ShapeDtypeStruct((total // unit * (unit + TAIL), width), jnp.bfloat16),
            jax.ShapeDtypeStruct((unit, width), jnp.float32),
        ],
        compiler_params=pltpu.CompilerParams(vmem_limit_bytes=VMEM_LIMIT),
        cost_estimate=pl.CostEstimate(flops=0, bytes_accessed=0, transcendentals=0),
    )(index, *terms, part, own, *back)


def finish_kernel(divisor, parts_ref, own_ref, pair_ref, *refs):
    if divisor is None:
        grad_ref, scalar_ref = refs
    else:
        other_ref, grad_ref, loss_ref = refs
    count = parts_ref.shape[0]
    rows = own_ref.shape[0]
    value = own_ref[...] - pair_ref[...].astype(jnp.float32)
    tail = jnp.zeros((TAIL, own_ref.shape[1]), jnp.float32)
    for part in range(count):
        value = value + parts_ref[part, :rows, :].astype(jnp.float32)
        tail = tail + parts_ref[part, rows:, :].astype(jnp.float32)
    grad_ref[...] = 100.0 * value
    if divisor is None:
        scalar_ref[...] = tail
    else:
        loss_ref[0] = jnp.sum(tail[0:1, :] + other_ref[0:1, :]) / divisor


def finished(parts, own, pair, scalars=None, divisor=None):
    vmem = pl.BlockSpec(memory_space=pltpu.VMEM)
    if divisor is None:
        last, place, given = jax.ShapeDtypeStruct((TAIL, own.shape[1]), jnp.float32), vmem, []
    else:
        last, place, given = jax.ShapeDtypeStruct((1,), jnp.float32), pl.BlockSpec(memory_space=pltpu.SMEM), [scalars]
    return pl.pallas_call(
        functools.partial(finish_kernel, divisor),
        in_specs=[vmem] * (3 + len(given)),
        out_specs=[vmem, place],
        out_shape=[jax.ShapeDtypeStruct(own.shape, jnp.float32), last],
        compiler_params=pltpu.CompilerParams(vmem_limit_bytes=VMEM_LIMIT),
    )(parts, own, pair, *given)


def bits_of(x, y, z):
    return {axis + kind: PAIRS[at][k] for axis, at in zip("xyz", (x, y, z)) for k, kind in enumerate("pq")}


def groups_of(names):
    found = {}
    for z, y, x, core in itertools.product(range(4), range(4), range(4), range(2)):
        bits = bits_of(x, y, z)
        key = tuple(bits[name] for name in sorted(bits) if name not in names) + (core,)
        place = functools.reduce(lambda total, name: 2 * total + bits[name], names, 0)
        found.setdefault(key, {})[place] = ((((z // 2) * 4 + y) * 4 + x) * 2 + z % 2) * 2 + core
    return [[group[place] for place in sorted(group)] for group in found.values()]


def own_bits():
    where = {"x": lax.axis_index("x"), "y": lax.axis_index("y"), "z": 2 * lax.axis_index("zh") + lax.axis_index("zl")}
    bits = {}
    for axis, at in where.items():
        bits[axis + "p"] = jnp.where((at == 1) | (at == 2), 1, 0)
        bits[axis + "q"] = at // 2
    return bits


def place_of(names, bits):
    return functools.reduce(lambda total, name: 2 * total + bits[name], names, 0)


def doubled(value, names, name, bits):
    mask = 1 << (len(names) - 1 - names.index(name))
    pairs = [(group[at], group[at ^ mask]) for group in groups_of(names) for at in range(len(group))]
    back = lax.ppermute(value, AXES, pairs)
    at = lax.broadcasted_iota(jnp.int32, (2,) + (1,) * value.ndim, 0)
    return jnp.where(at == bits[name], value[None], back[None])


def gathered(image, text, bits):
    half = image.shape[0] // 2
    pieces = [image[:half], image[half:], text[:half], text[half:]]
    names = [A_BITS, A_BITS, B_BITS, B_BITS]
    for turn in range(3):
        pieces = [
            doubled(piece, name, name[2 - turn] if k % 2 == 0 else name[2 - (2, 0, 1)[turn]], bits)
            for k, (piece, name) in enumerate(zip(pieces, names))
        ]
    whole = []
    for k in (0, 2):
        both = jnp.stack([pieces[k], jnp.transpose(pieces[k + 1], (2, 0, 1, 3, 4))], axis=3)
        whole.append(both.reshape(16 * half, image.shape[1]))
    return lax.optimization_barrier(tuple(whole))


def swap(value):
    return lax.ppermute(value, "c", [(0, 1), (1, 0)])


def exchanged(blocks, names):
    return lax.all_to_all(
        blocks, AXES, split_axis=0, concat_axis=0, tiled=True, axis_index_groups=groups_of(names)
    )


def joined(first, second):
    peak = jnp.maximum(first, second)
    return peak + jnp.log2(jnp.exp2(first - peak) + jnp.exp2(second - peak))


def body(image_embed, text_embed):
    rows, width = image_embed.shape
    bits = own_bits()
    members = 2 ** len(A_BITS)
    half = members * rows
    batch = rows * 2 * members * members
    at_a = jnp.full((1,), place_of(A_BITS, bits), jnp.int32)
    at_b = jnp.full((1,), place_of(B_BITS, bits), jnp.int32)

    own, text = gathered(image_embed, text_embed, bits)
    other = swap(own)
    row_part, col_parts = forward(own, other, text, image_embed, text_embed, members)

    col_parts = exchanged(col_parts, B_BITS)
    count = half // 128
    back = swap(row_part)
    row_part = joined(row_part, jnp.concatenate([back[count:], back[:count]], axis=0))
    row_parts = exchanged(jnp.broadcast_to(row_part[None], (members,) + row_part.shape), A_BITS)

    text_sum, text_own, col_lse, row_lse, term = text_gradient(text, own, other, col_parts, row_parts, rows, at_b)
    term_back = swap(term)
    text_sum, own, other = lax.optimization_barrier((text_sum, own, other))
    text_parts = exchanged(text_sum.reshape(members, rows + TAIL, width), B_BITS)
    image_mine, image_half, *image_other = image_gradient(own, other, text, row_lse, col_lse, rows, at_a)
    image_back = [swap(piece) for piece in image_other]
    image_sum, image_own = packed(image_mine, image_half, image_back, rows, at_a, (term, term_back))
    image_parts = exchanged(image_sum.reshape(members, rows + TAIL, width), A_BITS)
    text_grad, tail_b = finished(text_parts, text_own, image_embed)
    image_grad, mean_loss = finished(image_parts, image_own, text_embed, tail_b, 2.0 * batch)
    return (image_grad, text_grad, mean_loss)


def solution(mesh):
    fine = Mesh(mesh.devices.reshape(2, 4, 4, 2, 2), AXES)
    spec = P(AXES, None)
    return jax.shard_map(body, mesh=fine, in_specs=(spec, spec), out_specs=(spec, spec, P()), check_vma=False)
```

```python
import functools
import itertools
import math

import jax
import jax.numpy as jnp
from jax import lax
from jax.experimental import pallas as pl
from jax.experimental.pallas import tpu as pltpu
from jax.sharding import Mesh, PartitionSpec as P

AXES = ("zh", "y", "x", "zl", "c")
A_BITS = ("zp", "yq", "yp")
B_BITS = ("zq", "xq", "xp")
PAIRS = ((0, 0), (1, 0), (1, 1), (0, 1))
SWAP = [(0, 1), (1, 0)]
LOG2E = math.log2(math.e)
LN2 = math.log(2.0)
SCALE = 100.0 * LOG2E
BLOCK = 256
TAIL = 16
TEXT_BLOCKS = 1
PARTS = 4
VMEM_LIMIT = 56 * 1024 * 1024


def forward_kernel(own_ref, other_ref, text_ref, image_ref, pair_ref, row_ref, col_ref, text_t, scores, block_max, col_max, col_sum):
    half = own_ref.shape[0]
    columns = text_ref.shape[0]
    count = 2 * half // BLOCK
    text_t[...] = text_ref[...].T
    col_max[...] = jnp.full(col_max.shape, -1e30, jnp.float32)
    col_sum[...] = jnp.zeros(col_sum.shape, jnp.float32)

    def multiply(index, slot):
        piece, at = (own_ref, index * BLOCK) if index * BLOCK < half else (other_ref, index * BLOCK - half)
        rows = piece[at : at + BLOCK, :]
        for start in range(0, columns, BLOCK):
            cols = slice(start, start + BLOCK)
            part = SCALE * jnp.dot(rows, text_t[:, cols], preferred_element_type=jnp.float32)
            scores[slot][:, cols] = part
            block_max[slot][:, cols] = jnp.max(part.reshape(BLOCK // 8, 8, BLOCK), axis=0)

    def sums(index, slot):
        old = col_max[...]
        peak = jnp.maximum(old, block_max[slot][...])
        col_max[...] = peak
        total = col_sum[...] * jnp.exp2(old - peak)
        tops, parts = [], []
        for start in range(0, BLOCK, 8):
            block = scores[slot][start : start + 8, :]
            pieces = [block[:, k : k + 128] for k in range(0, columns, 128)]
            top = functools.reduce(jnp.maximum, pieces)
            tops.append(top)
            parts.append(functools.reduce(jnp.add, [jnp.exp2(piece - top) for piece in pieces]))
            total = total + jnp.exp2(block - peak)
        col_sum[...] = total
        tops = jnp.concatenate(tops, axis=0).T
        parts = jnp.concatenate(parts, axis=0).T
        top = jnp.max(tops, axis=0, keepdims=True)
        row_lse = top + jnp.log2(jnp.sum(parts * jnp.exp2(tops - top), axis=0, keepdims=True))
        for k in range(BLOCK // 128):
            at = index * (BLOCK // 128) + k
            row_ref[at : at + 1, :] = row_lse[:, k * 128 : k * 128 + 128]

    multiply(0, 0)

    for index in range(count):
        if index + 1 < count:
            multiply(index + 1, (index + 1) % 2)
        sums(index, index % 2)

    peak = jnp.max(col_max[...], axis=0, keepdims=True)
    total = jnp.sum(col_sum[...] * jnp.exp2(col_max[...] - peak), axis=0, keepdims=True)
    col_lse = peak + jnp.log2(total)
    products = image_ref[...].astype(jnp.float32) * pair_ref[...].astype(jnp.float32)
    diagonal = 100.0 * jnp.sum(jnp.sum(products, axis=0, keepdims=True), axis=1, keepdims=True)
    count = columns // 128
    for place in range(col_ref.shape[0]):
        for k in range(count):
            col_ref[place, k : k + 1, :] = col_lse[:, k * 128 : k * 128 + 128]
        col_ref[place, count:, :] = jnp.broadcast_to(diagonal, (col_ref.shape[1] - count, 128))


def forward(own, other, text, image, pair, members):
    half, width = own.shape
    columns = text.shape[0]
    elements = 2 * half * columns
    f32 = lambda *shape: pltpu.VMEM(shape, jnp.float32)
    return pl.pallas_call(
        forward_kernel,
        out_shape=[
            jax.ShapeDtypeStruct((2 * half // 128, 128), jnp.float32),
            jax.ShapeDtypeStruct((members, columns // 128 + 2, 128), jnp.float32),
        ],
        scratch_shapes=[
            pltpu.VMEM((width, columns), jnp.bfloat16),
            [f32(BLOCK, columns), f32(BLOCK, columns)],
            [f32(8, columns), f32(8, columns)],
            f32(8, columns),
            f32(8, columns),
        ],
        compiler_params=pltpu.CompilerParams(vmem_limit_bytes=VMEM_LIMIT),
        cost_estimate=pl.CostEstimate(
            flops=2 * elements * width, bytes_accessed=4 * (half + columns) * width, transcendentals=2 * elements
        ),
    )(own, other, text, image, pair)


def tail_of(scalar, width):
    spread = jnp.broadcast_to(scalar, (TAIL, width))
    high = spread.astype(jnp.bfloat16).astype(jnp.float32)
    middle = (spread - high).astype(jnp.bfloat16).astype(jnp.float32)
    low = spread - high - middle
    lane = lax.broadcasted_iota(jnp.int32, (TAIL, width), 1)
    values = jnp.where(lane == 0, high, jnp.where(lane == 1, middle, jnp.where(lane == 2, low, 0.0)))
    return values.astype(jnp.bfloat16)


def whole_lse(parts_ref, lse_ref):
    count = lse_ref.shape[1] // 128
    parts = parts_ref[:, :count, :]
    peak = jnp.max(parts, axis=0)
    value = peak + jnp.log2(jnp.sum(jnp.exp2(parts - peak[None]), axis=0)) + 1.0
    for k in range(count):
        lse_ref[:, k * 128 : k * 128 + 128] = jnp.broadcast_to(value[k : k + 1, :], (8, 128))


def gradient_kernel(unit, pack, *refs):
    if pack:
        index_ref, row_parts, col_parts, rows_ref, first_ref, second_ref, *refs = refs
        out_ref, own_ref, row_ref, col_ref, term_ref, *refs = refs
        whole_lse(row_parts, row_ref)
        whole_lse(col_parts, col_ref)
        lse_sum = jnp.sum(row_ref[0:1, :] - 1.0, axis=1, keepdims=True)
        diagonal = jnp.sum(row_parts[:, row_parts.shape[1] - 1, 0:1], axis=0, keepdims=True)
        term_ref[...] = jnp.broadcast_to(LN2 * lse_sum - 2.0 * diagonal, term_ref.shape)
        column_refs = (first_ref, second_ref)
    else:
        index_ref, row_ref, col_ref, own_rows, other_rows, column_ref, *refs = refs
        mine_ref, out_ref, *refs = refs
        other_refs, (rows_ref, *refs) = refs[:PARTS], refs[PARTS:]
        rows_ref[: other_rows.shape[0], :] = other_rows[...]
        rows_ref[other_rows.shape[0] :, :] = own_rows[...]
        column_refs = (column_ref,)
    columns_t, columns, scores, weights, row_lse, tail = refs
    total = rows_ref.shape[0]
    block = weights[0].shape[0]
    count = total // block
    size = column_refs[0].shape[0]
    for piece, column_ref in enumerate(column_refs):
        part = slice(piece * size, (piece + 1) * size)
        columns_t[:, part] = column_ref[...].T
        columns[part, :] = column_ref[...]
    across = columns.shape[0]
    if pack:
        row_lse[...] = jnp.broadcast_to(row_ref[0:1, :], (128, total)).T
        halves = [col_ref[0:1, : across // 2], col_ref[0:1, across // 2 :]]
        sums = [jnp.sum(half - 1.0, axis=1, keepdims=True) for half in halves]
        tail[...] = tail_of(LN2 * (sums[0] + sums[1]), tail.shape[1])
    else:
        row_lse[: total // 2, :] = jnp.broadcast_to(row_ref[0:1, total // 2 :], (128, total // 2)).T
        row_lse[total // 2 :, :] = jnp.broadcast_to(row_ref[0:1, : total // 2], (128, total // 2)).T

    def rows_at(index):
        if isinstance(index, int):
            return slice(index * block, (index + 1) * block)
        return pl.ds(pl.multiple_of(index * block, block), block)

    def multiply(index, slot):
        rows = rows_ref[rows_at(index), :]
        for start in range(0, across, BLOCK):
            cols = slice(start, start + BLOCK)
            scores[slot][:, cols] = jnp.dot(rows, columns_t[:, cols], preferred_element_type=jnp.float32)

    def weigh(index, slot):
        row_part = row_lse[rows_at(index), :]
        for start in range(0, across, 128):
            cols = slice(start, start + 128)
            scaled = SCALE * scores[slot][:, cols]
            value = jnp.exp2(scaled - row_part) + jnp.exp2(scaled - col_ref[0:1, cols])
            weights[slot][:, cols] = value.astype(jnp.bfloat16)

    def collect(index, slot):
        value = jnp.dot(weights[slot][...], columns[...], preferred_element_type=jnp.float32)
        if not pack:
            if index < PARTS:
                other_refs[index][...] = value.astype(out_ref.dtype)
                return
            out_ref[(index - PARTS) * block : (index - PARTS + 1) * block, :] = value.astype(out_ref.dtype)
            for part in range(block // unit):
                mine = (index - PARTS) * (block // unit) + part == index_ref[0]
                mine_ref[...] = jnp.where(mine, value[part * unit : (part + 1) * unit, :], mine_ref[...])
            return
        for part in range(block // unit):
            place = index * (block // unit) + part
            mine = place == index_ref[0]
            at = pl.multiple_of(place * (unit + TAIL), TAIL)
            piece = value[part * unit : (part + 1) * unit, :]
            out_ref[pl.ds(at, unit), :] = jnp.where(mine, 0.0, piece).astype(out_ref.dtype)
            out_ref[pl.ds(pl.multiple_of(at + unit, TAIL), TAIL), :] = tail[...]
            own_ref[...] = jnp.where(mine, piece, own_ref[...])

    multiply(0, 0)
    multiply(1, 1)
    weigh(0, 0)

    def turns(turn):
        multiply(2 * turn + 2, 0)
        collect(2 * turn, 0)
        weigh(2 * turn + 1, 1)
        multiply(2 * turn + 3, 1)
        collect(2 * turn + 1, 1)
        weigh(2 * turn + 2, 0)

    if pack:
        pl.loop(0, count // 2 - 1)(turns)
    else:
        for turn in range(count // 2 - 1):
            turns(turn)
    collect(count - 2, 0)
    weigh(count - 1, 1)
    collect(count - 1, 1)


def gradient_scratch(total, across, width, block):
    return [
        pltpu.VMEM((width, across), jnp.bfloat16),
        pltpu.VMEM((across, width), jnp.bfloat16),
        [pltpu.VMEM((block, across), jnp.float32)] * 2,
        [pltpu.VMEM((block, across), jnp.bfloat16)] * 2,
        pltpu.VMEM((total, 128), jnp.float32),
        pltpu.VMEM((TAIL, width), jnp.bfloat16),
    ]


def text_gradient(text, own, other, col_parts, row_parts, unit, index):
    total, width = text.shape
    across = 2 * own.shape[0]
    vmem = pl.BlockSpec(memory_space=pltpu.VMEM)
    return pl.pallas_call(
        functools.partial(gradient_kernel, unit, True),
        in_specs=[pl.BlockSpec(memory_space=pltpu.SMEM)] + [vmem] * 5,
        out_shape=[
            jax.ShapeDtypeStruct((total // unit * (unit + TAIL), width), jnp.bfloat16),
            jax.ShapeDtypeStruct((unit, width), jnp.float32),
            jax.ShapeDtypeStruct((8, total), jnp.float32),
            jax.ShapeDtypeStruct((8, across), jnp.float32),
            jax.ShapeDtypeStruct((8, 128), jnp.float32),
        ],
        scratch_shapes=gradient_scratch(total, across, width, TEXT_BLOCKS * unit),
        compiler_params=pltpu.CompilerParams(vmem_limit_bytes=VMEM_LIMIT),
        cost_estimate=pl.CostEstimate(
            flops=4 * total * across * width, bytes_accessed=4 * (total + across) * width, transcendentals=0
        ),
    )(index, col_parts, row_parts, text, own, other)


def image_gradient(own, other, text, row_lse, col_lse, unit, index):
    half, width = own.shape
    across = text.shape[0]
    block = half // PARTS
    return pl.pallas_call(
        functools.partial(gradient_kernel, unit, False),
        in_specs=[pl.BlockSpec(memory_space=pltpu.SMEM)] + [pl.BlockSpec(memory_space=pltpu.VMEM)] * 5,
        out_shape=[
            jax.ShapeDtypeStruct((unit, width), jnp.float32),
            jax.ShapeDtypeStruct((half, width), jnp.bfloat16),
        ]
        + [jax.ShapeDtypeStruct((block, width), jnp.bfloat16)] * PARTS,
        scratch_shapes=[pltpu.VMEM((2 * half, width), jnp.bfloat16)] + gradient_scratch(2 * half, across, width, block),
        compiler_params=pltpu.CompilerParams(vmem_limit_bytes=VMEM_LIMIT),
        cost_estimate=pl.CostEstimate(
            flops=0, bytes_accessed=0, transcendentals=0
        ),
    )(index, row_lse, col_lse, own, other, text)


def pack_kernel(index_ref, term_ref, term_back_ref, part_ref, own_ref, *refs):
    *back_refs, out_ref, mine_ref = refs
    unit = mine_ref.shape[0]
    size = back_refs[0].shape[0]
    tail = tail_of(term_ref[0:1, 0:1] + term_back_ref[0:1, 0:1], out_ref.shape[1])
    for place in range(own_ref.shape[0] // unit):
        part = slice(place * unit, (place + 1) * unit)
        mine = index_ref[0] == place
        start = place * unit % size
        back = back_refs[place * unit // size][start : start + unit, :]
        back = back.astype(jnp.float32)
        value = own_ref[part, :].astype(jnp.float32) + back
        at = place * (unit + TAIL)
        out_ref[at : at + unit, :] = jnp.where(mine, 0.0, value).astype(out_ref.dtype)
        out_ref[at + unit : at + unit + TAIL, :] = tail

        @pl.when(mine)
        def _():
            mine_ref[...] = part_ref[...] + back


def packed(part, own, back, unit, index, terms):
    total, width = own.shape
    smem = pl.BlockSpec(memory_space=pltpu.SMEM)
    vmem = pl.BlockSpec(memory_space=pltpu.VMEM)
    return pl.pallas_call(
        pack_kernel,
        in_specs=[smem] + [vmem] * (4 + len(back)),
        out_shape=[
            jax.ShapeDtypeStruct((total // unit * (unit + TAIL), width), jnp.bfloat16),
            jax.ShapeDtypeStruct((unit, width), jnp.float32),
        ],
        compiler_params=pltpu.CompilerParams(vmem_limit_bytes=VMEM_LIMIT),
        cost_estimate=pl.CostEstimate(flops=0, bytes_accessed=0, transcendentals=0),
    )(index, *terms, part, own, *back)


def finish_kernel(divisor, parts_ref, own_ref, pair_ref, *refs):
    if divisor is None:
        grad_ref, scalar_ref = refs
    else:
        other_ref, grad_ref, loss_ref = refs
    count = parts_ref.shape[0]
    rows = own_ref.shape[0]
    value = own_ref[...] - pair_ref[...].astype(jnp.float32)
    tail = jnp.zeros((TAIL, own_ref.shape[1]), jnp.float32)
    for part in range(count):
        value = value + parts_ref[part, :rows, :].astype(jnp.float32)
        tail = tail + parts_ref[part, rows:, :].astype(jnp.float32)
    grad_ref[...] = 100.0 * value
    if divisor is None:
        scalar_ref[...] = tail
    else:
        loss_ref[0] = jnp.sum(tail[0:1, :] + other_ref[0:1, :]) / divisor


def finished(parts, own, pair, scalars=None, divisor=None):
    vmem = pl.BlockSpec(memory_space=pltpu.VMEM)
    if divisor is None:
        last, place, given = jax.ShapeDtypeStruct((TAIL, own.shape[1]), jnp.float32), vmem, []
    else:
        last, place, given = jax.ShapeDtypeStruct((1,), jnp.float32), pl.BlockSpec(memory_space=pltpu.SMEM), [scalars]
    return pl.pallas_call(
        functools.partial(finish_kernel, divisor),
        in_specs=[vmem] * (3 + len(given)),
        out_specs=[vmem, place],
        out_shape=[jax.ShapeDtypeStruct(own.shape, jnp.float32), last],
        compiler_params=pltpu.CompilerParams(vmem_limit_bytes=VMEM_LIMIT),
    )(parts, own, pair, *given)


def bits_of(x, y, z):
    return {axis + kind: PAIRS[at][k] for axis, at in zip("xyz", (x, y, z)) for k, kind in enumerate("pq")}


def groups_of(names):
    found = {}
    for z, y, x, core in itertools.product(range(4), range(4), range(4), range(2)):
        bits = bits_of(x, y, z)
        key = tuple(bits[name] for name in sorted(bits) if name not in names) + (core,)
        place = functools.reduce(lambda total, name: 2 * total + bits[name], names, 0)
        found.setdefault(key, {})[place] = ((((z // 2) * 4 + y) * 4 + x) * 2 + z % 2) * 2 + core
    return [[group[place] for place in sorted(group)] for group in found.values()]


def own_bits():
    where = {"x": lax.axis_index("x"), "y": lax.axis_index("y"), "z": 2 * lax.axis_index("zh") + lax.axis_index("zl")}
    bits = {}
    for axis, at in where.items():
        bits[axis + "p"] = jnp.where((at == 1) | (at == 2), 1, 0)
        bits[axis + "q"] = at // 2
    return bits


def place_of(names, bits):
    return functools.reduce(lambda total, name: 2 * total + bits[name], names, 0)


def doubled(value, names, name, bits):
    mask = 1 << (len(names) - 1 - names.index(name))
    pairs = [(group[at], group[at ^ mask]) for group in groups_of(names) for at in range(len(group))]
    back = lax.ppermute(value, AXES, pairs)
    at = lax.broadcasted_iota(jnp.int32, (2,) + (1,) * value.ndim, 0)
    return jnp.where(at == bits[name], value[None], back[None])


def gathered(image, text, bits):
    half = image.shape[0] // 2
    pieces = [image[:half], image[half:], text[:half], text[half:]]
    names = [A_BITS, A_BITS, B_BITS, B_BITS]
    for turn in range(3):
        pieces = [
            doubled(piece, name, name[2 - turn] if k % 2 == 0 else name[2 - (2, 0, 1)[turn]], bits)
            for k, (piece, name) in enumerate(zip(pieces, names))
        ]
    whole = []
    for k in (0, 2):
        both = jnp.stack([pieces[k], jnp.transpose(pieces[k + 1], (2, 0, 1, 3, 4))], axis=3)
        whole.append(both.reshape(16 * half, image.shape[1]))
    return lax.optimization_barrier(tuple(whole))


def swap(value):
    return lax.ppermute(value, "c", [(0, 1), (1, 0)])


def exchanged(blocks, names):
    return lax.all_to_all(
        blocks, AXES, split_axis=0, concat_axis=0, tiled=True, axis_index_groups=groups_of(names)
    )


def joined(first, second):
    peak = jnp.maximum(first, second)
    return peak + jnp.log2(jnp.exp2(first - peak) + jnp.exp2(second - peak))


def body(image_embed, text_embed):
    rows, width = image_embed.shape
    bits = own_bits()
    members = 2 ** len(A_BITS)
    half = members * rows
    batch = rows * 2 * members * members
    at_a = jnp.full((1,), place_of(A_BITS, bits), jnp.int32)
    at_b = jnp.full((1,), place_of(B_BITS, bits), jnp.int32)

    own, text = gathered(image_embed, text_embed, bits)
    other = swap(own)
    row_part, col_parts = forward(own, other, text, image_embed, text_embed, members)

    col_parts = exchanged(col_parts, B_BITS)
    count = half // 128
    back = swap(row_part)
    row_part = joined(row_part, jnp.concatenate([back[count:], back[:count]], axis=0))
    row_parts = exchanged(jnp.broadcast_to(row_part[None], (members,) + row_part.shape), A_BITS)

    text_sum, text_own, col_lse, row_lse, term = text_gradient(text, own, other, col_parts, row_parts, rows, at_b)
    term_back = swap(term)
    text_sum, own, other = lax.optimization_barrier((text_sum, own, other))
    text_parts = exchanged(text_sum.reshape(members, rows + TAIL, width), B_BITS)
    image_mine, image_half, *image_other = image_gradient(own, other, text, row_lse, col_lse, rows, at_a)
    image_back = [swap(piece) for piece in image_other]
    image_sum, image_own = packed(image_mine, image_half, image_back, rows, at_a, (term, term_back))
    image_parts = exchanged(image_sum.reshape(members, rows + TAIL, width), A_BITS)
    text_grad, tail_b = finished(text_parts, text_own, image_embed)
    image_grad, mean_loss = finished(image_parts, image_own, text_embed, tail_b, 2.0 * batch)
    return (image_grad, text_grad, mean_loss)


def solution(mesh):
    fine = Mesh(mesh.devices.reshape(2, 4, 4, 2, 2), AXES)
    spec = P(AXES, None)
    return jax.shard_map(body, mesh=fine, in_specs=(spec, spec), out_specs=(spec, spec, P()), check_vma=False)
```

```python
import functools
import itertools
import math

import jax
import jax.numpy as jnp
from jax import lax
from jax.experimental import pallas as pl
from jax.experimental.pallas import tpu as pltpu
from jax.sharding import Mesh, PartitionSpec as P

AXES = ("zh", "y", "x", "zl", "c")
A_BITS = ("zp", "yq", "yp")
B_BITS = ("zq", "xq", "xp")
PAIRS = ((0, 0), (1, 0), (1, 1), (0, 1))
SWAP = [(0, 1), (1, 0)]
LOG2E = math.log2(math.e)
LN2 = math.log(2.0)
SCALE = 100.0 * LOG2E
BLOCK = 256
TAIL = 16
TEXT_BLOCKS = 1
PARTS = 4
VMEM_LIMIT = 56 * 1024 * 1024


def forward_kernel(own_ref, other_ref, text_ref, image_ref, pair_ref, row_ref, col_ref, text_t, image, scores, block_max, col_max, col_sum):
    half = own_ref.shape[0]
    columns = text_ref.shape[0]
    count = 2 * half // BLOCK
    text_t[...] = text_ref[...].T
    image[:half, :] = own_ref[...]
    image[half:, :] = other_ref[...]
    col_max[...] = jnp.full(col_max.shape, -1e30, jnp.float32)
    col_sum[...] = jnp.zeros(col_sum.shape, jnp.float32)

    def multiply(index, slot):
        at = pl.multiple_of(jnp.minimum(index, count - 1) * BLOCK, BLOCK)
        rows = image[pl.ds(at, BLOCK), :]
        for start in range(0, columns, BLOCK):
            cols = slice(start, start + BLOCK)
            part = SCALE * jnp.dot(rows, text_t[:, cols], preferred_element_type=jnp.float32)
            scores[slot][:, cols] = part
            block_max[slot][:, cols] = jnp.max(part.reshape(BLOCK // 8, 8, BLOCK), axis=0)

    def sums(index, slot):
        old = col_max[...]
        peak = jnp.maximum(old, block_max[slot][...])
        col_max[...] = peak
        total = col_sum[...] * jnp.exp2(old - peak)
        tops, parts = [], []
        for start in range(0, BLOCK, 8):
            block = scores[slot][start : start + 8, :]
            pieces = [block[:, k : k + 128] for k in range(0, columns, 128)]
            top = functools.reduce(jnp.maximum, pieces)
            tops.append(top)
            parts.append(functools.reduce(jnp.add, [jnp.exp2(piece - top) for piece in pieces]))
            total = total + jnp.exp2(block - peak)
        col_sum[...] = total
        tops = jnp.concatenate(tops, axis=0).T
        parts = jnp.concatenate(parts, axis=0).T
        top = jnp.max(tops, axis=0, keepdims=True)
        row_lse = top + jnp.log2(jnp.sum(parts * jnp.exp2(tops - top), axis=0, keepdims=True))
        for k in range(BLOCK // 128):
            row_ref[pl.ds(index * (BLOCK // 128) + k, 1), :] = row_lse[:, k * 128 : k * 128 + 128]

    multiply(0, 0)

    @pl.loop(0, count // 2)
    def _(turn):
        multiply(2 * turn + 1, 1)
        sums(2 * turn, 0)
        multiply(2 * turn + 2, 0)
        sums(2 * turn + 1, 1)

    peak = jnp.max(col_max[...], axis=0, keepdims=True)
    total = jnp.sum(col_sum[...] * jnp.exp2(col_max[...] - peak), axis=0, keepdims=True)
    col_lse = peak + jnp.log2(total)
    products = image_ref[...].astype(jnp.float32) * pair_ref[...].astype(jnp.float32)
    diagonal = 100.0 * jnp.sum(jnp.sum(products, axis=0, keepdims=True), axis=1, keepdims=True)
    count = columns // 128
    for place in range(col_ref.shape[0]):
        for k in range(count):
            col_ref[place, k : k + 1, :] = col_lse[:, k * 128 : k * 128 + 128]
        col_ref[place, count:, :] = jnp.broadcast_to(diagonal, (col_ref.shape[1] - count, 128))


def forward(own, other, text, image, pair, members):
    half, width = own.shape
    columns = text.shape[0]
    elements = 2 * half * columns
    f32 = lambda *shape: pltpu.VMEM(shape, jnp.float32)
    return pl.pallas_call(
        forward_kernel,
        out_shape=[
            jax.ShapeDtypeStruct((2 * half // 128, 128), jnp.float32),
            jax.ShapeDtypeStruct((members, columns // 128 + 2, 128), jnp.float32),
        ],
        scratch_shapes=[
            pltpu.VMEM((width, columns), jnp.bfloat16),
            pltpu.VMEM((2 * half, width), jnp.bfloat16),
            [f32(BLOCK, columns), f32(BLOCK, columns)],
            [f32(8, columns), f32(8, columns)],
            f32(8, columns),
            f32(8, columns),
        ],
        compiler_params=pltpu.CompilerParams(vmem_limit_bytes=VMEM_LIMIT),
        cost_estimate=pl.CostEstimate(
            flops=2 * elements * width, bytes_accessed=4 * (half + columns) * width, transcendentals=2 * elements
        ),
    )(own, other, text, image, pair)


def tail_of(scalar, width):
    spread = jnp.broadcast_to(scalar, (TAIL, width))
    high = spread.astype(jnp.bfloat16).astype(jnp.float32)
    middle = (spread - high).astype(jnp.bfloat16).astype(jnp.float32)
    low = spread - high - middle
    lane = lax.broadcasted_iota(jnp.int32, (TAIL, width), 1)
    values = jnp.where(lane == 0, high, jnp.where(lane == 1, middle, jnp.where(lane == 2, low, 0.0)))
    return values.astype(jnp.bfloat16)


def whole_lse(parts_ref, lse_ref):
    count = lse_ref.shape[1] // 128
    parts = parts_ref[:, :count, :]
    peak = jnp.max(parts, axis=0)
    value = peak + jnp.log2(jnp.sum(jnp.exp2(parts - peak[None]), axis=0)) + 1.0
    for k in range(count):
        lse_ref[:, k * 128 : k * 128 + 128] = jnp.broadcast_to(value[k : k + 1, :], (8, 128))


def gradient_kernel(unit, pack, *refs):
    if pack:
        index_ref, row_parts, col_parts, rows_ref, first_ref, second_ref, *refs = refs
        out_ref, own_ref, row_ref, col_ref, term_ref, *refs = refs
        whole_lse(row_parts, row_ref)
        whole_lse(col_parts, col_ref)
        lse_sum = jnp.sum(row_ref[0:1, :] - 1.0, axis=1, keepdims=True)
        diagonal = jnp.sum(row_parts[:, row_parts.shape[1] - 1, 0:1], axis=0, keepdims=True)
        term_ref[...] = jnp.broadcast_to(LN2 * lse_sum - 2.0 * diagonal, term_ref.shape)
        column_refs = (first_ref, second_ref)
    else:
        index_ref, row_ref, col_ref, own_rows, other_rows, column_ref, *refs = refs
        mine_ref, out_ref, *refs = refs
        other_refs, (rows_ref, *refs) = refs[:PARTS], refs[PARTS:]
        rows_ref[: other_rows.shape[0], :] = other_rows[...]
        rows_ref[other_rows.shape[0] :, :] = own_rows[...]
        column_refs = (column_ref,)
    columns_t, columns, scores, weights, row_lse, tail = refs
    total = rows_ref.shape[0]
    block = weights[0].shape[0]
    count = total // block
    size = column_refs[0].shape[0]
    for piece, column_ref in enumerate(column_refs):
        part = slice(piece * size, (piece + 1) * size)
        columns_t[:, part] = column_ref[...].T
        columns[part, :] = column_ref[...]
    across = columns.shape[0]
    if pack:
        row_lse[...] = jnp.broadcast_to(row_ref[0:1, :], (128, total)).T
        halves = [col_ref[0:1, : across // 2], col_ref[0:1, across // 2 :]]
        sums = [jnp.sum(half - 1.0, axis=1, keepdims=True) for half in halves]
        tail[...] = tail_of(LN2 * (sums[0] + sums[1]), tail.shape[1])
    else:
        row_lse[: total // 2, :] = jnp.broadcast_to(row_ref[0:1, total // 2 :], (128, total // 2)).T
        row_lse[total // 2 :, :] = jnp.broadcast_to(row_ref[0:1, : total // 2], (128, total // 2)).T

    def rows_at(index):
        if isinstance(index, int):
            return slice(index * block, (index + 1) * block)
        return pl.ds(pl.multiple_of(index * block, block), block)

    def multiply(index, slot):
        rows = rows_ref[rows_at(index), :]
        for start in range(0, across, BLOCK):
            cols = slice(start, start + BLOCK)
            scores[slot][:, cols] = jnp.dot(rows, columns_t[:, cols], preferred_element_type=jnp.float32)

    def weigh(index, slot):
        row_part = row_lse[rows_at(index), :]
        for start in range(0, across, 128):
            cols = slice(start, start + 128)
            scaled = SCALE * scores[slot][:, cols]
            value = jnp.exp2(scaled - row_part) + jnp.exp2(scaled - col_ref[0:1, cols])
            weights[slot][:, cols] = value.astype(jnp.bfloat16)

    def collect(index, slot):
        value = jnp.dot(weights[slot][...], columns[...], preferred_element_type=jnp.float32)
        if not pack:
            if index < PARTS:
                other_refs[index][...] = value.astype(out_ref.dtype)
                return
            out_ref[(index - PARTS) * block : (index - PARTS + 1) * block, :] = value.astype(out_ref.dtype)
            for part in range(block // unit):
                mine = (index - PARTS) * (block // unit) + part == index_ref[0]
                mine_ref[...] = jnp.where(mine, value[part * unit : (part + 1) * unit, :], mine_ref[...])
            return
        for part in range(block // unit):
            place = index * (block // unit) + part
            mine = place == index_ref[0]
            at = pl.multiple_of(place * (unit + TAIL), TAIL)
            piece = value[part * unit : (part + 1) * unit, :]
            out_ref[pl.ds(at, unit), :] = jnp.where(mine, 0.0, piece).astype(out_ref.dtype)
            out_ref[pl.ds(pl.multiple_of(at + unit, TAIL), TAIL), :] = tail[...]
            own_ref[...] = jnp.where(mine, piece, own_ref[...])

    multiply(0, 0)
    multiply(1, 1)
    weigh(0, 0)

    def turns(turn):
        multiply(2 * turn + 2, 0)
        collect(2 * turn, 0)
        weigh(2 * turn + 1, 1)
        multiply(2 * turn + 3, 1)
        collect(2 * turn + 1, 1)
        weigh(2 * turn + 2, 0)

    if pack:
        pl.loop(0, count // 2 - 1)(turns)
    else:
        for turn in range(count // 2 - 1):
            turns(turn)
    collect(count - 2, 0)
    weigh(count - 1, 1)
    collect(count - 1, 1)


def gradient_scratch(total, across, width, block):
    return [
        pltpu.VMEM((width, across), jnp.bfloat16),
        pltpu.VMEM((across, width), jnp.bfloat16),
        [pltpu.VMEM((block, across), jnp.float32)] * 2,
        [pltpu.VMEM((block, across), jnp.bfloat16)] * 2,
        pltpu.VMEM((total, 128), jnp.float32),
        pltpu.VMEM((TAIL, width), jnp.bfloat16),
    ]


def text_gradient(text, own, other, col_parts, row_parts, unit, index):
    total, width = text.shape
    across = 2 * own.shape[0]
    vmem = pl.BlockSpec(memory_space=pltpu.VMEM)
    return pl.pallas_call(
        functools.partial(gradient_kernel, unit, True),
        in_specs=[pl.BlockSpec(memory_space=pltpu.SMEM)] + [vmem] * 5,
        out_shape=[
            jax.ShapeDtypeStruct((total // unit * (unit + TAIL), width), jnp.bfloat16),
            jax.ShapeDtypeStruct((unit, width), jnp.float32),
            jax.ShapeDtypeStruct((8, total), jnp.float32),
            jax.ShapeDtypeStruct((8, across), jnp.float32),
            jax.ShapeDtypeStruct((8, 128), jnp.float32),
        ],
        scratch_shapes=gradient_scratch(total, across, width, TEXT_BLOCKS * unit),
        compiler_params=pltpu.CompilerParams(vmem_limit_bytes=VMEM_LIMIT),
        cost_estimate=pl.CostEstimate(
            flops=4 * total * across * width, bytes_accessed=4 * (total + across) * width, transcendentals=0
        ),
    )(index, col_parts, row_parts, text, own, other)


def image_gradient(own, other, text, row_lse, col_lse, unit, index):
    half, width = own.shape
    across = text.shape[0]
    block = half // PARTS
    return pl.pallas_call(
        functools.partial(gradient_kernel, unit, False),
        in_specs=[pl.BlockSpec(memory_space=pltpu.SMEM)] + [pl.BlockSpec(memory_space=pltpu.VMEM)] * 5,
        out_shape=[
            jax.ShapeDtypeStruct((unit, width), jnp.float32),
            jax.ShapeDtypeStruct((half, width), jnp.bfloat16),
        ]
        + [jax.ShapeDtypeStruct((block, width), jnp.bfloat16)] * PARTS,
        scratch_shapes=[pltpu.VMEM((2 * half, width), jnp.bfloat16)] + gradient_scratch(2 * half, across, width, block),
        compiler_params=pltpu.CompilerParams(vmem_limit_bytes=VMEM_LIMIT),
        cost_estimate=pl.CostEstimate(
            flops=0, bytes_accessed=0, transcendentals=0
        ),
    )(index, row_lse, col_lse, own, other, text)


def pack_kernel(index_ref, term_ref, term_back_ref, part_ref, own_ref, *refs):
    *back_refs, out_ref, mine_ref = refs
    unit = mine_ref.shape[0]
    size = back_refs[0].shape[0]
    tail = tail_of(term_ref[0:1, 0:1] + term_back_ref[0:1, 0:1], out_ref.shape[1])
    for place in range(own_ref.shape[0] // unit):
        part = slice(place * unit, (place + 1) * unit)
        mine = index_ref[0] == place
        start = place * unit % size
        back = back_refs[place * unit // size][start : start + unit, :]
        back = back.astype(jnp.float32)
        value = own_ref[part, :].astype(jnp.float32) + back
        at = place * (unit + TAIL)
        out_ref[at : at + unit, :] = jnp.where(mine, 0.0, value).astype(out_ref.dtype)
        out_ref[at + unit : at + unit + TAIL, :] = tail

        @pl.when(mine)
        def _():
            mine_ref[...] = part_ref[...] + back


def packed(part, own, back, unit, index, terms):
    total, width = own.shape
    smem = pl.BlockSpec(memory_space=pltpu.SMEM)
    vmem = pl.BlockSpec(memory_space=pltpu.VMEM)
    return pl.pallas_call(
        pack_kernel,
        in_specs=[smem] + [vmem] * (4 + len(back)),
        out_shape=[
            jax.ShapeDtypeStruct((total // unit * (unit + TAIL), width), jnp.bfloat16),
            jax.ShapeDtypeStruct((unit, width), jnp.float32),
        ],
        compiler_params=pltpu.CompilerParams(vmem_limit_bytes=VMEM_LIMIT),
        cost_estimate=pl.CostEstimate(flops=0, bytes_accessed=0, transcendentals=0),
    )(index, *terms, part, own, *back)


def finish_kernel(divisor, parts_ref, own_ref, pair_ref, *refs):
    if divisor is None:
        grad_ref, scalar_ref = refs
    else:
        other_ref, grad_ref, loss_ref = refs
    count = parts_ref.shape[0]
    rows = own_ref.shape[0]
    value = own_ref[...] - pair_ref[...].astype(jnp.float32)
    tail = jnp.zeros((TAIL, own_ref.shape[1]), jnp.float32)
    for part in range(count):
        value = value + parts_ref[part, :rows, :].astype(jnp.float32)
        tail = tail + parts_ref[part, rows:, :].astype(jnp.float32)
    grad_ref[...] = 100.0 * value
    if divisor is None:
        scalar_ref[...] = tail
    else:
        loss_ref[0] = jnp.sum(tail[0:1, :] + other_ref[0:1, :]) / divisor


def finished(parts, own, pair, scalars=None, divisor=None):
    vmem = pl.BlockSpec(memory_space=pltpu.VMEM)
    if divisor is None:
        last, place, given = jax.ShapeDtypeStruct((TAIL, own.shape[1]), jnp.float32), vmem, []
    else:
        last, place, given = jax.ShapeDtypeStruct((1,), jnp.float32), pl.BlockSpec(memory_space=pltpu.SMEM), [scalars]
    return pl.pallas_call(
        functools.partial(finish_kernel, divisor),
        in_specs=[vmem] * (3 + len(given)),
        out_specs=[vmem, place],
        out_shape=[jax.ShapeDtypeStruct(own.shape, jnp.float32), last],
        compiler_params=pltpu.CompilerParams(vmem_limit_bytes=VMEM_LIMIT),
    )(parts, own, pair, *given)


def bits_of(x, y, z):
    return {axis + kind: PAIRS[at][k] for axis, at in zip("xyz", (x, y, z)) for k, kind in enumerate("pq")}


def groups_of(names):
    found = {}
    for z, y, x, core in itertools.product(range(4), range(4), range(4), range(2)):
        bits = bits_of(x, y, z)
        key = tuple(bits[name] for name in sorted(bits) if name not in names) + (core,)
        place = functools.reduce(lambda total, name: 2 * total + bits[name], names, 0)
        found.setdefault(key, {})[place] = ((((z // 2) * 4 + y) * 4 + x) * 2 + z % 2) * 2 + core
    return [[group[place] for place in sorted(group)] for group in found.values()]


def own_bits():
    where = {"x": lax.axis_index("x"), "y": lax.axis_index("y"), "z": 2 * lax.axis_index("zh") + lax.axis_index("zl")}
    bits = {}
    for axis, at in where.items():
        bits[axis + "p"] = jnp.where((at == 1) | (at == 2), 1, 0)
        bits[axis + "q"] = at // 2
    return bits


def place_of(names, bits):
    return functools.reduce(lambda total, name: 2 * total + bits[name], names, 0)


def doubled(value, names, name, bits):
    mask = 1 << (len(names) - 1 - names.index(name))
    pairs = [(group[at], group[at ^ mask]) for group in groups_of(names) for at in range(len(group))]
    back = lax.ppermute(value, AXES, pairs)
    at = lax.broadcasted_iota(jnp.int32, (2,) + (1,) * value.ndim, 0)
    return jnp.where(at == bits[name], value[None], back[None])


def gathered(image, text, bits):
    half = image.shape[0] // 2
    pieces = [image[:half], image[half:], text[:half], text[half:]]
    names = [A_BITS, A_BITS, B_BITS, B_BITS]
    for turn in range(3):
        pieces = [
            doubled(piece, name, name[2 - turn] if k % 2 == 0 else name[2 - (2, 0, 1)[turn]], bits)
            for k, (piece, name) in enumerate(zip(pieces, names))
        ]
    whole = []
    for k in (0, 2):
        both = jnp.stack([pieces[k], jnp.transpose(pieces[k + 1], (2, 0, 1, 3, 4))], axis=3)
        whole.append(both.reshape(16 * half, image.shape[1]))
    return lax.optimization_barrier(tuple(whole))


def swap(value):
    return lax.ppermute(value, "c", [(0, 1), (1, 0)])


def exchanged(blocks, names):
    return lax.all_to_all(
        blocks, AXES, split_axis=0, concat_axis=0, tiled=True, axis_index_groups=groups_of(names)
    )


def joined(first, second):
    peak = jnp.maximum(first, second)
    return peak + jnp.log2(jnp.exp2(first - peak) + jnp.exp2(second - peak))


def body(image_embed, text_embed):
    rows, width = image_embed.shape
    bits = own_bits()
    members = 2 ** len(A_BITS)
    half = members * rows
    batch = rows * 2 * members * members
    at_a = jnp.full((1,), place_of(A_BITS, bits), jnp.int32)
    at_b = jnp.full((1,), place_of(B_BITS, bits), jnp.int32)

    own, text = gathered(image_embed, text_embed, bits)
    other = swap(own)
    row_part, col_parts = forward(own, other, text, image_embed, text_embed, members)

    col_parts = exchanged(col_parts, B_BITS)
    count = half // 128
    back = swap(row_part)
    row_part = joined(row_part, jnp.concatenate([back[count:], back[:count]], axis=0))
    row_parts = exchanged(jnp.broadcast_to(row_part[None], (members,) + row_part.shape), A_BITS)

    text_sum, text_own, col_lse, row_lse, term = text_gradient(text, own, other, col_parts, row_parts, rows, at_b)
    term_back = swap(term)
    text_sum, own, other = lax.optimization_barrier((text_sum, own, other))
    text_parts = exchanged(text_sum.reshape(members, rows + TAIL, width), B_BITS)
    image_mine, image_half, *image_other = image_gradient(own, other, text, row_lse, col_lse, rows, at_a)
    image_back = [swap(piece) for piece in image_other]
    image_sum, image_own = packed(image_mine, image_half, image_back, rows, at_a, (term, term_back))
    image_parts = exchanged(image_sum.reshape(members, rows + TAIL, width), A_BITS)
    text_grad, tail_b = finished(text_parts, text_own, image_embed)
    image_grad, mean_loss = finished(image_parts, image_own, text_embed, tail_b, 2.0 * batch)
    return (image_grad, text_grad, mean_loss)


def solution(mesh):
    fine = Mesh(mesh.devices.reshape(2, 4, 4, 2, 2), AXES)
    spec = P(AXES, None)
    return jax.shard_map(body, mesh=fine, in_specs=(spec, spec), out_specs=(spec, spec, P()), check_vma=False)
```

```python
import functools
import itertools
import math

import jax
import jax.numpy as jnp
from jax import lax
from jax.experimental import pallas as pl
from jax.experimental.pallas import tpu as pltpu
from jax.sharding import Mesh, PartitionSpec as P

AXES = ("zh", "y", "x", "zl", "c")
A_BITS = ("zp", "yq", "yp")
B_BITS = ("zq", "xq", "xp")
PAIRS = ((0, 0), (1, 0), (1, 1), (0, 1))
SWAP = [(0, 1), (1, 0)]
LOG2E = math.log2(math.e)
LN2 = math.log(2.0)
SCALE = 100.0 * LOG2E
BLOCK = 256
TAIL = 16
TEXT_BLOCKS = 1
PARTS = 4
VMEM_LIMIT = 56 * 1024 * 1024


def forward_kernel(own_ref, other_ref, text_ref, image_ref, pair_ref, row_ref, col_ref, text_t, image, scores, block_max, row_max, row_sum, col_max, col_sum):
    half = own_ref.shape[0]
    columns = text_ref.shape[0]
    count = 2 * half // BLOCK
    text_t[...] = text_ref[...].T
    image[:half, :] = own_ref[...]
    image[half:, :] = other_ref[...]
    col_max[...] = jnp.full(col_max.shape, -1e30, jnp.float32)
    col_sum[...] = jnp.zeros(col_sum.shape, jnp.float32)

    def multiply(index, slot):
        at = pl.multiple_of(jnp.minimum(index, count - 1) * BLOCK, BLOCK)
        rows = image[pl.ds(at, BLOCK), :]
        for start in range(0, columns, BLOCK):
            cols = slice(start, start + BLOCK)
            part = SCALE * jnp.dot(rows, text_t[:, cols], preferred_element_type=jnp.float32)
            scores[slot][:, cols] = part
            block_max[slot][:, cols] = jnp.max(part.reshape(BLOCK // 8, 8, BLOCK), axis=0)

    def sums(index, slot):
        old = col_max[...]
        peak = jnp.maximum(old, block_max[slot][...])
        col_max[...] = peak
        total = col_sum[...] * jnp.exp2(old - peak)
        for start in range(0, BLOCK, 8):
            block = scores[slot][start : start + 8, :]
            pieces = [block[:, k : k + 128] for k in range(0, columns, 128)]
            top = functools.reduce(jnp.maximum, pieces)
            at = pl.multiple_of(index * BLOCK + start, 8)
            row_max[pl.ds(at, 8), :] = top
            row_sum[pl.ds(at, 8), :] = functools.reduce(jnp.add, [jnp.exp2(piece - top) for piece in pieces])
            total = total + jnp.exp2(block - peak)
        col_sum[...] = total

    multiply(0, 0)

    @pl.loop(0, count // 2)
    def _(turn):
        multiply(2 * turn + 1, 1)
        sums(2 * turn, 0)
        multiply(2 * turn + 2, 0)
        sums(2 * turn + 1, 1)

    tops = row_max[...].T
    parts = row_sum[...].T
    peak = jnp.max(tops, axis=0, keepdims=True)
    total = jnp.sum(parts * jnp.exp2(tops - peak), axis=0, keepdims=True)
    row_lse = peak + jnp.log2(total)
    for k in range(2 * half // 128):
        row_ref[k : k + 1, :] = row_lse[:, k * 128 : k * 128 + 128]
    peak = jnp.max(col_max[...], axis=0, keepdims=True)
    total = jnp.sum(col_sum[...] * jnp.exp2(col_max[...] - peak), axis=0, keepdims=True)
    col_lse = peak + jnp.log2(total)
    products = image_ref[...].astype(jnp.float32) * pair_ref[...].astype(jnp.float32)
    diagonal = 100.0 * jnp.sum(jnp.sum(products, axis=0, keepdims=True), axis=1, keepdims=True)
    count = columns // 128
    for place in range(col_ref.shape[0]):
        for k in range(count):
            col_ref[place, k : k + 1, :] = col_lse[:, k * 128 : k * 128 + 128]
        col_ref[place, count:, :] = jnp.broadcast_to(diagonal, (col_ref.shape[1] - count, 128))


def forward(own, other, text, image, pair, members):
    half, width = own.shape
    columns = text.shape[0]
    elements = 2 * half * columns
    f32 = lambda *shape: pltpu.VMEM(shape, jnp.float32)
    return pl.pallas_call(
        forward_kernel,
        out_shape=[
            jax.ShapeDtypeStruct((2 * half // 128, 128), jnp.float32),
            jax.ShapeDtypeStruct((members, columns // 128 + 2, 128), jnp.float32),
        ],
        scratch_shapes=[
            pltpu.VMEM((width, columns), jnp.bfloat16),
            pltpu.VMEM((2 * half, width), jnp.bfloat16),
            [f32(BLOCK, columns), f32(BLOCK, columns)],
            [f32(8, columns), f32(8, columns)],
            f32(2 * half, 128),
            f32(2 * half, 128),
            f32(8, columns),
            f32(8, columns),
        ],
        compiler_params=pltpu.CompilerParams(vmem_limit_bytes=VMEM_LIMIT),
        cost_estimate=pl.CostEstimate(
            flops=2 * elements * width, bytes_accessed=4 * (half + columns) * width, transcendentals=2 * elements
        ),
    )(own, other, text, image, pair)


def tail_of(scalar, width):
    spread = jnp.broadcast_to(scalar, (TAIL, width))
    high = spread.astype(jnp.bfloat16).astype(jnp.float32)
    middle = (spread - high).astype(jnp.bfloat16).astype(jnp.float32)
    low = spread - high - middle
    lane = lax.broadcasted_iota(jnp.int32, (TAIL, width), 1)
    values = jnp.where(lane == 0, high, jnp.where(lane == 1, middle, jnp.where(lane == 2, low, 0.0)))
    return values.astype(jnp.bfloat16)


def whole_lse(parts_ref, lse_ref):
    count = lse_ref.shape[1] // 128
    parts = parts_ref[:, :count, :]
    peak = jnp.max(parts, axis=0)
    value = peak + jnp.log2(jnp.sum(jnp.exp2(parts - peak[None]), axis=0)) + 1.0
    for k in range(count):
        lse_ref[:, k * 128 : k * 128 + 128] = jnp.broadcast_to(value[k : k + 1, :], (8, 128))


def gradient_kernel(unit, pack, *refs):
    if pack:
        index_ref, row_parts, col_parts, rows_ref, first_ref, second_ref, *refs = refs
        out_ref, own_ref, row_ref, col_ref, term_ref, *refs = refs
        whole_lse(row_parts, row_ref)
        whole_lse(col_parts, col_ref)
        lse_sum = jnp.sum(row_ref[0:1, :] - 1.0, axis=1, keepdims=True)
        diagonal = jnp.sum(row_parts[:, row_parts.shape[1] - 1, 0:1], axis=0, keepdims=True)
        term_ref[...] = jnp.broadcast_to(LN2 * lse_sum - 2.0 * diagonal, term_ref.shape)
        column_refs = (first_ref, second_ref)
    else:
        index_ref, row_ref, col_ref, own_rows, other_rows, column_ref, *refs = refs
        mine_ref, out_ref, *refs = refs
        other_refs, (rows_ref, *refs) = refs[:PARTS], refs[PARTS:]
        rows_ref[: other_rows.shape[0], :] = other_rows[...]
        rows_ref[other_rows.shape[0] :, :] = own_rows[...]
        column_refs = (column_ref,)
    columns_t, columns, scores, weights, row_lse, tail = refs
    total = rows_ref.shape[0]
    block = weights[0].shape[0]
    count = total // block
    size = column_refs[0].shape[0]
    for piece, column_ref in enumerate(column_refs):
        part = slice(piece * size, (piece + 1) * size)
        columns_t[:, part] = column_ref[...].T
        columns[part, :] = column_ref[...]
    across = columns.shape[0]
    if pack:
        row_lse[...] = jnp.broadcast_to(row_ref[0:1, :], (128, total)).T
        halves = [col_ref[0:1, : across // 2], col_ref[0:1, across // 2 :]]
        sums = [jnp.sum(half - 1.0, axis=1, keepdims=True) for half in halves]
        tail[...] = tail_of(LN2 * (sums[0] + sums[1]), tail.shape[1])
    else:
        row_lse[: total // 2, :] = jnp.broadcast_to(row_ref[0:1, total // 2 :], (128, total // 2)).T
        row_lse[total // 2 :, :] = jnp.broadcast_to(row_ref[0:1, : total // 2], (128, total // 2)).T

    def rows_at(index):
        if isinstance(index, int):
            return slice(index * block, (index + 1) * block)
        return pl.ds(pl.multiple_of(index * block, block), block)

    def multiply(index, slot):
        rows = rows_ref[rows_at(index), :]
        for start in range(0, across, BLOCK):
            cols = slice(start, start + BLOCK)
            scores[slot][:, cols] = jnp.dot(rows, columns_t[:, cols], preferred_element_type=jnp.float32)

    def weigh(index, slot):
        row_part = row_lse[rows_at(index), :]
        for start in range(0, across, 128):
            cols = slice(start, start + 128)
            scaled = SCALE * scores[slot][:, cols]
            value = jnp.exp2(scaled - row_part) + jnp.exp2(scaled - col_ref[0:1, cols])
            weights[slot][:, cols] = value.astype(jnp.bfloat16)

    def collect(index, slot):
        value = jnp.dot(weights[slot][...], columns[...], preferred_element_type=jnp.float32)
        if not pack:
            if index < PARTS:
                other_refs[index][...] = value.astype(out_ref.dtype)
                return
            out_ref[(index - PARTS) * block : (index - PARTS + 1) * block, :] = value.astype(out_ref.dtype)
            for part in range(block // unit):
                mine = (index - PARTS) * (block // unit) + part == index_ref[0]
                mine_ref[...] = jnp.where(mine, value[part * unit : (part + 1) * unit, :], mine_ref[...])
            return
        for part in range(block // unit):
            place = index * (block // unit) + part
            mine = place == index_ref[0]
            at = pl.multiple_of(place * (unit + TAIL), TAIL)
            piece = value[part * unit : (part + 1) * unit, :]
            out_ref[pl.ds(at, unit), :] = jnp.where(mine, 0.0, piece).astype(out_ref.dtype)
            out_ref[pl.ds(pl.multiple_of(at + unit, TAIL), TAIL), :] = tail[...]
            own_ref[...] = jnp.where(mine, piece, own_ref[...])

    multiply(0, 0)
    multiply(1, 1)
    weigh(0, 0)

    def turns(turn):
        multiply(2 * turn + 2, 0)
        collect(2 * turn, 0)
        weigh(2 * turn + 1, 1)
        multiply(2 * turn + 3, 1)
        collect(2 * turn + 1, 1)
        weigh(2 * turn + 2, 0)

    if pack:
        pl.loop(0, count // 2 - 1)(turns)
    else:
        for turn in range(count // 2 - 1):
            turns(turn)
    collect(count - 2, 0)
    weigh(count - 1, 1)
    collect(count - 1, 1)


def gradient_scratch(total, across, width, block):
    return [
        pltpu.VMEM((width, across), jnp.bfloat16),
        pltpu.VMEM((across, width), jnp.bfloat16),
        [pltpu.VMEM((block, across), jnp.float32)] * 2,
        [pltpu.VMEM((block, across), jnp.bfloat16)] * 2,
        pltpu.VMEM((total, 128), jnp.float32),
        pltpu.VMEM((TAIL, width), jnp.bfloat16),
    ]


def text_gradient(text, own, other, col_parts, row_parts, unit, index):
    total, width = text.shape
    across = 2 * own.shape[0]
    vmem = pl.BlockSpec(memory_space=pltpu.VMEM)
    return pl.pallas_call(
        functools.partial(gradient_kernel, unit, True),
        in_specs=[pl.BlockSpec(memory_space=pltpu.SMEM)] + [vmem] * 5,
        out_shape=[
            jax.ShapeDtypeStruct((total // unit * (unit + TAIL), width), jnp.bfloat16),
            jax.ShapeDtypeStruct((unit, width), jnp.float32),
            jax.ShapeDtypeStruct((8, total), jnp.float32),
            jax.ShapeDtypeStruct((8, across), jnp.float32),
            jax.ShapeDtypeStruct((8, 128), jnp.float32),
        ],
        scratch_shapes=gradient_scratch(total, across, width, TEXT_BLOCKS * unit),
        compiler_params=pltpu.CompilerParams(vmem_limit_bytes=VMEM_LIMIT),
        cost_estimate=pl.CostEstimate(
            flops=4 * total * across * width, bytes_accessed=4 * (total + across) * width, transcendentals=0
        ),
    )(index, col_parts, row_parts, text, own, other)


def image_gradient(own, other, text, row_lse, col_lse, unit, index):
    half, width = own.shape
    across = text.shape[0]
    block = half // PARTS
    return pl.pallas_call(
        functools.partial(gradient_kernel, unit, False),
        in_specs=[pl.BlockSpec(memory_space=pltpu.SMEM)] + [pl.BlockSpec(memory_space=pltpu.VMEM)] * 5,
        out_shape=[
            jax.ShapeDtypeStruct((unit, width), jnp.float32),
            jax.ShapeDtypeStruct((half, width), jnp.bfloat16),
        ]
        + [jax.ShapeDtypeStruct((block, width), jnp.bfloat16)] * PARTS,
        scratch_shapes=[pltpu.VMEM((2 * half, width), jnp.bfloat16)] + gradient_scratch(2 * half, across, width, block),
        compiler_params=pltpu.CompilerParams(vmem_limit_bytes=VMEM_LIMIT),
        cost_estimate=pl.CostEstimate(
            flops=0, bytes_accessed=0, transcendentals=0
        ),
    )(index, row_lse, col_lse, own, other, text)


def pack_kernel(index_ref, term_ref, term_back_ref, part_ref, own_ref, *refs):
    *back_refs, out_ref, mine_ref = refs
    unit = mine_ref.shape[0]
    size = back_refs[0].shape[0]
    tail = tail_of(term_ref[0:1, 0:1] + term_back_ref[0:1, 0:1], out_ref.shape[1])
    for place in range(own_ref.shape[0] // unit):
        part = slice(place * unit, (place + 1) * unit)
        mine = index_ref[0] == place
        start = place * unit % size
        back = back_refs[place * unit // size][start : start + unit, :]
        back = back.astype(jnp.float32)
        value = own_ref[part, :].astype(jnp.float32) + back
        at = place * (unit + TAIL)
        out_ref[at : at + unit, :] = jnp.where(mine, 0.0, value).astype(out_ref.dtype)
        out_ref[at + unit : at + unit + TAIL, :] = tail

        @pl.when(mine)
        def _():
            mine_ref[...] = part_ref[...] + back


def packed(part, own, back, unit, index, terms):
    total, width = own.shape
    smem = pl.BlockSpec(memory_space=pltpu.SMEM)
    vmem = pl.BlockSpec(memory_space=pltpu.VMEM)
    return pl.pallas_call(
        pack_kernel,
        in_specs=[smem] + [vmem] * (4 + len(back)),
        out_shape=[
            jax.ShapeDtypeStruct((total // unit * (unit + TAIL), width), jnp.bfloat16),
            jax.ShapeDtypeStruct((unit, width), jnp.float32),
        ],
        compiler_params=pltpu.CompilerParams(vmem_limit_bytes=VMEM_LIMIT),
        cost_estimate=pl.CostEstimate(flops=0, bytes_accessed=0, transcendentals=0),
    )(index, *terms, part, own, *back)


def finish_kernel(divisor, parts_ref, own_ref, pair_ref, *refs):
    if divisor is None:
        grad_ref, scalar_ref = refs
    else:
        other_ref, grad_ref, loss_ref = refs
    count = parts_ref.shape[0]
    rows = own_ref.shape[0]
    value = own_ref[...] - pair_ref[...].astype(jnp.float32)
    tail = jnp.zeros((TAIL, own_ref.shape[1]), jnp.float32)
    for part in range(count):
        value = value + parts_ref[part, :rows, :].astype(jnp.float32)
        tail = tail + parts_ref[part, rows:, :].astype(jnp.float32)
    grad_ref[...] = 100.0 * value
    if divisor is None:
        scalar_ref[...] = tail
    else:
        loss_ref[0] = jnp.sum(tail[0:1, :] + other_ref[0:1, :]) / divisor


def finished(parts, own, pair, scalars=None, divisor=None):
    vmem = pl.BlockSpec(memory_space=pltpu.VMEM)
    if divisor is None:
        last, place, given = jax.ShapeDtypeStruct((TAIL, own.shape[1]), jnp.float32), vmem, []
    else:
        last, place, given = jax.ShapeDtypeStruct((1,), jnp.float32), pl.BlockSpec(memory_space=pltpu.SMEM), [scalars]
    return pl.pallas_call(
        functools.partial(finish_kernel, divisor),
        in_specs=[vmem] * (3 + len(given)),
        out_specs=[vmem, place],
        out_shape=[jax.ShapeDtypeStruct(own.shape, jnp.float32), last],
        compiler_params=pltpu.CompilerParams(vmem_limit_bytes=VMEM_LIMIT),
    )(parts, own, pair, *given)


def bits_of(x, y, z):
    return {axis + kind: PAIRS[at][k] for axis, at in zip("xyz", (x, y, z)) for k, kind in enumerate("pq")}


def groups_of(names):
    found = {}
    for z, y, x, core in itertools.product(range(4), range(4), range(4), range(2)):
        bits = bits_of(x, y, z)
        key = tuple(bits[name] for name in sorted(bits) if name not in names) + (core,)
        place = functools.reduce(lambda total, name: 2 * total + bits[name], names, 0)
        found.setdefault(key, {})[place] = ((((z // 2) * 4 + y) * 4 + x) * 2 + z % 2) * 2 + core
    return [[group[place] for place in sorted(group)] for group in found.values()]


def own_bits():
    where = {"x": lax.axis_index("x"), "y": lax.axis_index("y"), "z": 2 * lax.axis_index("zh") + lax.axis_index("zl")}
    bits = {}
    for axis, at in where.items():
        bits[axis + "p"] = jnp.where((at == 1) | (at == 2), 1, 0)
        bits[axis + "q"] = at // 2
    return bits


def place_of(names, bits):
    return functools.reduce(lambda total, name: 2 * total + bits[name], names, 0)


def doubled(value, names, name, bits):
    back = partner(value, names, name)
    at = lax.broadcasted_iota(jnp.int32, (2,) + (1,) * value.ndim, 0)
    return jnp.where(at == bits[name], value[None], back[None])


def gathered(image, text, bits):
    half = image.shape[0] // 2
    pieces = [image[:half], image[half:], text[:half], text[half:]]
    names = [A_BITS, A_BITS, B_BITS, B_BITS]
    for turn in range(3):
        pieces = [
            doubled(piece, name, name[2 - turn] if k % 2 == 0 else name[2 - (2, 0, 1)[turn]], bits)
            for k, (piece, name) in enumerate(zip(pieces, names))
        ]
    whole = []
    for k in (0, 2):
        both = jnp.stack([pieces[k], jnp.transpose(pieces[k + 1], (2, 0, 1, 3, 4))], axis=3)
        whole.append(both.reshape(16 * half, image.shape[1]))
    return lax.optimization_barrier(tuple(whole))


def partner(value, names, name):
    mask = 1 << (len(names) - 1 - names.index(name))
    pairs = [(group[at], group[at ^ mask]) for group in groups_of(names) for at in range(len(group))]
    return lax.ppermute(value, AXES, pairs)


def swap(value):
    return lax.ppermute(value, "c", [(0, 1), (1, 0)])


def exchanged(blocks, names):
    return lax.all_to_all(
        blocks, AXES, split_axis=0, concat_axis=0, tiled=True, axis_index_groups=groups_of(names)
    )


def joined(first, second):
    peak = jnp.maximum(first, second)
    return peak + jnp.log2(jnp.exp2(first - peak) + jnp.exp2(second - peak))


def body(image_embed, text_embed):
    rows, width = image_embed.shape
    bits = own_bits()
    members = 2 ** len(A_BITS)
    half = members * rows
    batch = rows * 2 * members * members
    at_a = jnp.full((1,), place_of(A_BITS, bits), jnp.int32)
    at_b = jnp.full((1,), place_of(B_BITS, bits), jnp.int32)

    own, text = gathered(image_embed, text_embed, bits)
    other = swap(own)
    row_part, col_parts = forward(own, other, text, image_embed, text_embed, 1)

    count = half // 128
    kind = lax.broadcasted_iota(jnp.int32, col_parts.shape, 1)
    for name in B_BITS:
        back = partner(col_parts, B_BITS, name)
        col_parts = jnp.where(kind < count, joined(col_parts, back), col_parts + back)
    back = swap(row_part)
    row_part = joined(row_part, jnp.concatenate([back[count:], back[:count]], axis=0))
    row_parts = exchanged(jnp.broadcast_to(row_part[None], (members,) + row_part.shape), A_BITS)

    text_sum, text_own, col_lse, row_lse, term = text_gradient(text, own, other, col_parts, row_parts, rows, at_b)
    term_back = swap(term)
    text_sum, own, other = lax.optimization_barrier((text_sum, own, other))
    text_parts = exchanged(text_sum.reshape(members, rows + TAIL, width), B_BITS)
    image_mine, image_half, *image_other = image_gradient(own, other, text, row_lse, col_lse, rows, at_a)
    image_back = [swap(piece) for piece in image_other]
    image_sum, image_own = packed(image_mine, image_half, image_back, rows, at_a, (term, term_back))
    image_parts = exchanged(image_sum.reshape(members, rows + TAIL, width), A_BITS)
    text_grad, tail_b = finished(text_parts, text_own, image_embed)
    image_grad, mean_loss = finished(image_parts, image_own, text_embed, tail_b, 2.0 * batch)
    return (image_grad, text_grad, mean_loss)


def solution(mesh):
    fine = Mesh(mesh.devices.reshape(2, 4, 4, 2, 2), AXES)
    spec = P(AXES, None)
    return jax.shard_map(body, mesh=fine, in_specs=(spec, spec), out_specs=(spec, spec, P()), check_vma=False)
```

```python
import functools
import itertools
import math

import jax
import jax.numpy as jnp
from jax import lax
from jax.experimental import pallas as pl
from jax.experimental.pallas import tpu as pltpu
from jax.sharding import Mesh, PartitionSpec as P

AXES = ("zh", "y", "x", "zl", "c")
A_BITS = ("zp", "yq", "yp")
B_BITS = ("zq", "xq", "xp")
PAIRS = ((0, 0), (1, 0), (1, 1), (0, 1))
SWAP = [(0, 1), (1, 0)]
LOG2E = math.log2(math.e)
LN2 = math.log(2.0)
SCALE = 100.0 * LOG2E
BLOCK = 256
TAIL = 16
TEXT_BLOCKS = 1
PARTS = 4
VMEM_LIMIT = 56 * 1024 * 1024


def forward_kernel(own_ref, other_ref, text_ref, image_ref, pair_ref, row_ref, col_ref, text_t, image, scores, block_max, row_max, row_sum, col_max, col_sum):
    half = own_ref.shape[0]
    columns = text_ref.shape[0]
    count = 2 * half // BLOCK
    text_t[...] = text_ref[...].T
    image[:half, :] = own_ref[...]
    image[half:, :] = other_ref[...]
    col_max[...] = jnp.full(col_max.shape, -1e30, jnp.float32)
    col_sum[...] = jnp.zeros(col_sum.shape, jnp.float32)

    def multiply(index, slot):
        at = pl.multiple_of(jnp.minimum(index, count - 1) * BLOCK, BLOCK)
        rows = image[pl.ds(at, BLOCK), :]
        for start in range(0, columns, BLOCK):
            cols = slice(start, start + BLOCK)
            part = SCALE * jnp.dot(rows, text_t[:, cols], preferred_element_type=jnp.float32)
            scores[slot][:, cols] = part
            block_max[slot][:, cols] = jnp.max(part.reshape(BLOCK // 8, 8, BLOCK), axis=0)

    def sums(index, slot):
        old = col_max[...]
        peak = jnp.maximum(old, block_max[slot][...])
        col_max[...] = peak
        total = col_sum[...] * jnp.exp2(old - peak)
        for start in range(0, BLOCK, 8):
            block = scores[slot][start : start + 8, :]
            pieces = [block[:, k : k + 128] for k in range(0, columns, 128)]
            top = functools.reduce(jnp.maximum, pieces)
            at = pl.multiple_of(index * BLOCK + start, 8)
            row_max[pl.ds(at, 8), :] = top
            row_sum[pl.ds(at, 8), :] = functools.reduce(jnp.add, [jnp.exp2(piece - top) for piece in pieces])
            total = total + jnp.exp2(block - peak)
        col_sum[...] = total

    multiply(0, 0)

    @pl.loop(0, count // 2)
    def _(turn):
        multiply(2 * turn + 1, 1)
        sums(2 * turn, 0)
        multiply(2 * turn + 2, 0)
        sums(2 * turn + 1, 1)

    tops = row_max[...].T
    parts = row_sum[...].T
    peak = jnp.max(tops, axis=0, keepdims=True)
    total = jnp.sum(parts * jnp.exp2(tops - peak), axis=0, keepdims=True)
    row_lse = peak + jnp.log2(total)
    for k in range(2 * half // 128):
        row_ref[k : k + 1, :] = row_lse[:, k * 128 : k * 128 + 128]
    peak = jnp.max(col_max[...], axis=0, keepdims=True)
    total = jnp.sum(col_sum[...] * jnp.exp2(col_max[...] - peak), axis=0, keepdims=True)
    col_lse = peak + jnp.log2(total)
    products = image_ref[...].astype(jnp.float32) * pair_ref[...].astype(jnp.float32)
    diagonal = 100.0 * jnp.sum(jnp.sum(products, axis=0, keepdims=True), axis=1, keepdims=True)
    count = columns // 128
    for place in range(col_ref.shape[0]):
        for k in range(count):
            col_ref[place, k : k + 1, :] = col_lse[:, k * 128 : k * 128 + 128]
        col_ref[place, count:, :] = jnp.broadcast_to(diagonal, (col_ref.shape[1] - count, 128))


def forward(own, other, text, image, pair, members):
    half, width = own.shape
    columns = text.shape[0]
    elements = 2 * half * columns
    f32 = lambda *shape: pltpu.VMEM(shape, jnp.float32)
    return pl.pallas_call(
        forward_kernel,
        out_shape=[
            jax.ShapeDtypeStruct((2 * half // 128, 128), jnp.float32),
            jax.ShapeDtypeStruct((members, columns // 128 + 2, 128), jnp.float32),
        ],
        scratch_shapes=[
            pltpu.VMEM((width, columns), jnp.bfloat16),
            pltpu.VMEM((2 * half, width), jnp.bfloat16),
            [f32(BLOCK, columns), f32(BLOCK, columns)],
            [f32(8, columns), f32(8, columns)],
            f32(2 * half, 128),
            f32(2 * half, 128),
            f32(8, columns),
            f32(8, columns),
        ],
        compiler_params=pltpu.CompilerParams(vmem_limit_bytes=VMEM_LIMIT),
        cost_estimate=pl.CostEstimate(
            flops=2 * elements * width, bytes_accessed=4 * (half + columns) * width, transcendentals=2 * elements
        ),
    )(own, other, text, image, pair)


def tail_of(scalar, width):
    spread = jnp.broadcast_to(scalar, (TAIL, width))
    high = spread.astype(jnp.bfloat16).astype(jnp.float32)
    middle = (spread - high).astype(jnp.bfloat16).astype(jnp.float32)
    low = spread - high - middle
    lane = lax.broadcasted_iota(jnp.int32, (TAIL, width), 1)
    values = jnp.where(lane == 0, high, jnp.where(lane == 1, middle, jnp.where(lane == 2, low, 0.0)))
    return values.astype(jnp.bfloat16)


def whole_lse(parts_ref, lse_ref):
    count = lse_ref.shape[1] // 128
    parts = parts_ref[:, :count, :]
    peak = jnp.max(parts, axis=0)
    value = peak + jnp.log2(jnp.sum(jnp.exp2(parts - peak[None]), axis=0)) + 1.0
    for k in range(count):
        lse_ref[:, k * 128 : k * 128 + 128] = jnp.broadcast_to(value[k : k + 1, :], (8, 128))


def gradient_kernel(unit, pack, *refs):
    if pack:
        index_ref, row_parts, col_parts, rows_ref, first_ref, second_ref, *refs = refs
        out_ref, own_ref, row_ref, col_ref, term_ref, *refs = refs
        whole_lse(row_parts, row_ref)
        whole_lse(col_parts, col_ref)
        lse_sum = jnp.sum(row_ref[0:1, :] - 1.0, axis=1, keepdims=True)
        diagonal = jnp.sum(row_parts[:, row_parts.shape[1] - 1, 0:1], axis=0, keepdims=True)
        term_ref[...] = jnp.broadcast_to(LN2 * lse_sum - 2.0 * diagonal, term_ref.shape)
        column_refs = (first_ref, second_ref)
    else:
        index_ref, row_ref, col_ref, own_rows, other_rows, column_ref, *refs = refs
        mine_ref, out_ref, *refs = refs
        other_refs, (rows_ref, *refs) = refs[:PARTS], refs[PARTS:]
        rows_ref[: other_rows.shape[0], :] = other_rows[...]
        rows_ref[other_rows.shape[0] :, :] = own_rows[...]
        column_refs = (column_ref,)
    columns_t, columns, scores, weights, row_lse, tail = refs
    total = rows_ref.shape[0]
    block = weights[0].shape[0]
    count = total // block
    size = column_refs[0].shape[0]
    for piece, column_ref in enumerate(column_refs):
        part = slice(piece * size, (piece + 1) * size)
        columns_t[:, part] = column_ref[...].T
        columns[part, :] = column_ref[...]
    across = columns.shape[0]
    if pack:
        row_lse[...] = jnp.broadcast_to(row_ref[0:1, :], (128, total)).T
        halves = [col_ref[0:1, : across // 2], col_ref[0:1, across // 2 :]]
        sums = [jnp.sum(half - 1.0, axis=1, keepdims=True) for half in halves]
        tail[...] = tail_of(LN2 * (sums[0] + sums[1]), tail.shape[1])
    else:
        row_lse[: total // 2, :] = jnp.broadcast_to(row_ref[0:1, total // 2 :], (128, total // 2)).T
        row_lse[total // 2 :, :] = jnp.broadcast_to(row_ref[0:1, : total // 2], (128, total // 2)).T

    def rows_at(index):
        if isinstance(index, int):
            return slice(index * block, (index + 1) * block)
        return pl.ds(pl.multiple_of(index * block, block), block)

    def multiply(index, slot):
        rows = rows_ref[rows_at(index), :]
        for start in range(0, across, BLOCK):
            cols = slice(start, start + BLOCK)
            scores[slot][:, cols] = jnp.dot(rows, columns_t[:, cols], preferred_element_type=jnp.float32)

    def weigh(index, slot):
        row_part = row_lse[rows_at(index), :]
        for start in range(0, across, 128):
            cols = slice(start, start + 128)
            scaled = SCALE * scores[slot][:, cols]
            value = jnp.exp2(scaled - row_part) + jnp.exp2(scaled - col_ref[0:1, cols])
            weights[slot][:, cols] = value.astype(jnp.bfloat16)

    def collect(index, slot):
        value = jnp.dot(weights[slot][...], columns[...], preferred_element_type=jnp.float32)
        if not pack:
            if index < PARTS:
                other_refs[index][...] = value.astype(out_ref.dtype)
                return
            out_ref[(index - PARTS) * block : (index - PARTS + 1) * block, :] = value.astype(out_ref.dtype)
            for part in range(block // unit):
                mine = (index - PARTS) * (block // unit) + part == index_ref[0]
                mine_ref[...] = jnp.where(mine, value[part * unit : (part + 1) * unit, :], mine_ref[...])
            return
        for part in range(block // unit):
            place = index * (block // unit) + part
            mine = place == index_ref[0]
            at = pl.multiple_of(place * (unit + TAIL), TAIL)
            piece = value[part * unit : (part + 1) * unit, :]
            out_ref[pl.ds(at, unit), :] = jnp.where(mine, 0.0, piece).astype(out_ref.dtype)
            out_ref[pl.ds(pl.multiple_of(at + unit, TAIL), TAIL), :] = tail[...]
            own_ref[...] = jnp.where(mine, piece, own_ref[...])

    multiply(0, 0)
    multiply(1, 1)
    weigh(0, 0)

    def turns(turn):
        multiply(2 * turn + 2, 0)
        collect(2 * turn, 0)
        weigh(2 * turn + 1, 1)
        multiply(2 * turn + 3, 1)
        collect(2 * turn + 1, 1)
        weigh(2 * turn + 2, 0)

    if pack:
        pl.loop(0, count // 2 - 1)(turns)
    else:
        for turn in range(count // 2 - 1):
            turns(turn)
    collect(count - 2, 0)
    weigh(count - 1, 1)
    collect(count - 1, 1)


def gradient_scratch(total, across, width, block):
    return [
        pltpu.VMEM((width, across), jnp.bfloat16),
        pltpu.VMEM((across, width), jnp.bfloat16),
        [pltpu.VMEM((block, across), jnp.float32)] * 2,
        [pltpu.VMEM((block, across), jnp.bfloat16)] * 2,
        pltpu.VMEM((total, 128), jnp.float32),
        pltpu.VMEM((TAIL, width), jnp.bfloat16),
    ]


def text_gradient(text, own, other, col_parts, row_parts, unit, index):
    total, width = text.shape
    across = 2 * own.shape[0]
    vmem = pl.BlockSpec(memory_space=pltpu.VMEM)
    return pl.pallas_call(
        functools.partial(gradient_kernel, unit, True),
        in_specs=[pl.BlockSpec(memory_space=pltpu.SMEM)] + [vmem] * 5,
        out_shape=[
            jax.ShapeDtypeStruct((total // unit * (unit + TAIL), width), jnp.bfloat16),
            jax.ShapeDtypeStruct((unit, width), jnp.float32),
            jax.ShapeDtypeStruct((8, total), jnp.float32),
            jax.ShapeDtypeStruct((8, across), jnp.float32),
            jax.ShapeDtypeStruct((8, 128), jnp.float32),
        ],
        scratch_shapes=gradient_scratch(total, across, width, TEXT_BLOCKS * unit),
        compiler_params=pltpu.CompilerParams(vmem_limit_bytes=VMEM_LIMIT),
        cost_estimate=pl.CostEstimate(
            flops=4 * total * across * width, bytes_accessed=4 * (total + across) * width, transcendentals=0
        ),
    )(index, col_parts, row_parts, text, own, other)


def image_gradient(own, other, text, row_lse, col_lse, unit, index):
    half, width = own.shape
    across = text.shape[0]
    block = half // PARTS
    return pl.pallas_call(
        functools.partial(gradient_kernel, unit, False),
        in_specs=[pl.BlockSpec(memory_space=pltpu.SMEM)] + [pl.BlockSpec(memory_space=pltpu.VMEM)] * 5,
        out_shape=[
            jax.ShapeDtypeStruct((unit, width), jnp.float32),
            jax.ShapeDtypeStruct((half, width), jnp.bfloat16),
        ]
        + [jax.ShapeDtypeStruct((block, width), jnp.bfloat16)] * PARTS,
        scratch_shapes=[pltpu.VMEM((2 * half, width), jnp.bfloat16)] + gradient_scratch(2 * half, across, width, block),
        compiler_params=pltpu.CompilerParams(vmem_limit_bytes=VMEM_LIMIT),
        cost_estimate=pl.CostEstimate(
            flops=0, bytes_accessed=0, transcendentals=0
        ),
    )(index, row_lse, col_lse, own, other, text)


def pack_kernel(index_ref, term_ref, term_back_ref, part_ref, own_ref, *refs):
    *back_refs, out_ref, mine_ref = refs
    unit = mine_ref.shape[0]
    size = back_refs[0].shape[0]
    tail = tail_of(term_ref[0:1, 0:1] + term_back_ref[0:1, 0:1], out_ref.shape[1])
    for place in range(own_ref.shape[0] // unit):
        part = slice(place * unit, (place + 1) * unit)
        mine = index_ref[0] == place
        start = place * unit % size
        back = back_refs[place * unit // size][start : start + unit, :]
        back = back.astype(jnp.float32)
        value = own_ref[part, :].astype(jnp.float32) + back
        at = place * (unit + TAIL)
        out_ref[at : at + unit, :] = jnp.where(mine, 0.0, value).astype(out_ref.dtype)
        out_ref[at + unit : at + unit + TAIL, :] = tail

        @pl.when(mine)
        def _():
            mine_ref[...] = part_ref[...] + back


def packed(part, own, back, unit, index, terms):
    total, width = own.shape
    smem = pl.BlockSpec(memory_space=pltpu.SMEM)
    vmem = pl.BlockSpec(memory_space=pltpu.VMEM)
    return pl.pallas_call(
        pack_kernel,
        in_specs=[smem] + [vmem] * (4 + len(back)),
        out_shape=[
            jax.ShapeDtypeStruct((total // unit * (unit + TAIL), width), jnp.bfloat16),
            jax.ShapeDtypeStruct((unit, width), jnp.float32),
        ],
        compiler_params=pltpu.CompilerParams(vmem_limit_bytes=VMEM_LIMIT),
        cost_estimate=pl.CostEstimate(flops=0, bytes_accessed=0, transcendentals=0),
    )(index, *terms, part, own, *back)


def finish_kernel(divisor, parts_ref, own_ref, pair_ref, *refs):
    if divisor is None:
        grad_ref, scalar_ref = refs
    else:
        other_ref, grad_ref, loss_ref = refs
    count = parts_ref.shape[0]
    rows = own_ref.shape[0]
    value = own_ref[...] - pair_ref[...].astype(jnp.float32)
    tail = jnp.zeros((TAIL, own_ref.shape[1]), jnp.float32)
    for part in range(count):
        value = value + parts_ref[part, :rows, :].astype(jnp.float32)
        tail = tail + parts_ref[part, rows:, :].astype(jnp.float32)
    grad_ref[...] = 100.0 * value
    if divisor is None:
        scalar_ref[...] = tail
    else:
        loss_ref[0] = jnp.sum(tail[0:1, :] + other_ref[0:1, :]) / divisor


def finished(parts, own, pair, scalars=None, divisor=None):
    vmem = pl.BlockSpec(memory_space=pltpu.VMEM)
    if divisor is None:
        last, place, given = jax.ShapeDtypeStruct((TAIL, own.shape[1]), jnp.float32), vmem, []
    else:
        last, place, given = jax.ShapeDtypeStruct((1,), jnp.float32), pl.BlockSpec(memory_space=pltpu.SMEM), [scalars]
    return pl.pallas_call(
        functools.partial(finish_kernel, divisor),
        in_specs=[vmem] * (3 + len(given)),
        out_specs=[vmem, place],
        out_shape=[jax.ShapeDtypeStruct(own.shape, jnp.float32), last],
        compiler_params=pltpu.CompilerParams(vmem_limit_bytes=VMEM_LIMIT),
    )(parts, own, pair, *given)


def bits_of(x, y, z):
    return {axis + kind: PAIRS[at][k] for axis, at in zip("xyz", (x, y, z)) for k, kind in enumerate("pq")}


def groups_of(names):
    found = {}
    for z, y, x, core in itertools.product(range(4), range(4), range(4), range(2)):
        bits = bits_of(x, y, z)
        key = tuple(bits[name] for name in sorted(bits) if name not in names) + (core,)
        place = functools.reduce(lambda total, name: 2 * total + bits[name], names, 0)
        found.setdefault(key, {})[place] = ((((z // 2) * 4 + y) * 4 + x) * 2 + z % 2) * 2 + core
    return [[group[place] for place in sorted(group)] for group in found.values()]


def own_bits():
    where = {"x": lax.axis_index("x"), "y": lax.axis_index("y"), "z": 2 * lax.axis_index("zh") + lax.axis_index("zl")}
    bits = {}
    for axis, at in where.items():
        bits[axis + "p"] = jnp.where((at == 1) | (at == 2), 1, 0)
        bits[axis + "q"] = at // 2
    return bits


def place_of(names, bits):
    return functools.reduce(lambda total, name: 2 * total + bits[name], names, 0)


def doubled(value, names, name, bits):
    back = partner(value, names, name)
    at = lax.broadcasted_iota(jnp.int32, (2,) + (1,) * value.ndim, 0)
    return jnp.where(at == bits[name], value[None], back[None])


def gathered(image, text, bits):
    half = image.shape[0] // 2
    pieces = [image[:half], image[half:], text[:half], text[half:]]
    names = [A_BITS, A_BITS, B_BITS, B_BITS]
    for turn in range(3):
        pieces = [
            doubled(piece, name, name[2 - turn] if k % 2 == 0 else name[2 - (2, 0, 1)[turn]], bits)
            for k, (piece, name) in enumerate(zip(pieces, names))
        ]
    whole = []
    for k in (0, 2):
        both = jnp.stack([pieces[k], jnp.transpose(pieces[k + 1], (2, 0, 1, 3, 4))], axis=3)
        whole.append(both.reshape(16 * half, image.shape[1]))
    return lax.optimization_barrier(tuple(whole))


def partner(value, names, name):
    mask = 1 << (len(names) - 1 - names.index(name))
    pairs = [(group[at], group[at ^ mask]) for group in groups_of(names) for at in range(len(group))]
    return lax.ppermute(value, AXES, pairs)


def swap(value):
    return lax.ppermute(value, "c", [(0, 1), (1, 0)])


def exchanged(blocks, names):
    return lax.all_to_all(
        blocks, AXES, split_axis=0, concat_axis=0, tiled=True, axis_index_groups=groups_of(names)
    )


def joined(first, second):
    peak = jnp.maximum(first, second)
    return peak + jnp.log2(jnp.exp2(first - peak) + jnp.exp2(second - peak))


def body(image_embed, text_embed):
    rows, width = image_embed.shape
    bits = own_bits()
    members = 2 ** len(A_BITS)
    half = members * rows
    batch = rows * 2 * members * members
    at_a = jnp.full((1,), place_of(A_BITS, bits), jnp.int32)
    at_b = jnp.full((1,), place_of(B_BITS, bits), jnp.int32)

    own, text = gathered(image_embed, text_embed, bits)
    other = swap(own)
    row_part, col_parts = forward(own, other, text, image_embed, text_embed, 1)

    count = half // 128
    kind = lax.broadcasted_iota(jnp.int32, col_parts.shape, 1)
    for name in B_BITS:
        back = partner(col_parts, B_BITS, name)
        col_parts = jnp.where(kind < count, joined(col_parts, back), col_parts + back)
    row_parts = exchanged(jnp.broadcast_to(row_part[None], (members,) + row_part.shape), A_BITS)
    peak = jnp.max(row_parts, axis=0)
    row_part = peak + jnp.log2(jnp.sum(jnp.exp2(row_parts - peak[None]), axis=0))
    back = swap(row_part)
    row_parts = joined(row_part, jnp.concatenate([back[count:], back[:count]], axis=0))[None]

    text_sum, text_own, col_lse, row_lse, term = text_gradient(text, own, other, col_parts, row_parts, rows, at_b)
    term_back = swap(term)
    text_sum, own, other = lax.optimization_barrier((text_sum, own, other))
    text_parts = exchanged(text_sum.reshape(members, rows + TAIL, width), B_BITS)
    image_mine, image_half, *image_other = image_gradient(own, other, text, row_lse, col_lse, rows, at_a)
    image_back = [swap(piece) for piece in image_other]
    image_sum, image_own = packed(image_mine, image_half, image_back, rows, at_a, (term, term_back))
    image_parts = exchanged(image_sum.reshape(members, rows + TAIL, width), A_BITS)
    text_grad, tail_b = finished(text_parts, text_own, image_embed)
    image_grad, mean_loss = finished(image_parts, image_own, text_embed, tail_b, 2.0 * batch)
    return (image_grad, text_grad, mean_loss)


def solution(mesh):
    fine = Mesh(mesh.devices.reshape(2, 4, 4, 2, 2), AXES)
    spec = P(AXES, None)
    return jax.shard_map(body, mesh=fine, in_specs=(spec, spec), out_specs=(spec, spec, P()), check_vma=False)
```
